32 devices in a mesh: dp: 16 (over z, y, x), tensor: 2 (over core).
Axes of the slice: x: 2, y: 2, z: 4, core: 2. Of those that a mesh axis runs over, the one named last changes fastest.
Arguments:
- tokens: bfloat16 [32768, 768], P('dp', 'tensor'), may hold values from -6 to 6
- qkv_weight: bfloat16 [3, 768, 768], P(None, None, 'tensor'), may hold values from -0.21875 to 0.21875
- qv_bias: float32 [2, 768], P(None, 'tensor'), may hold values from -1.75 to 1.75
- out_weight: bfloat16 [768, 768], P('tensor'), may hold values from -0.875 to 0.875
- out_bias: float32 [768], P('tensor'), may hold values from -1.75 to 1.75
- first_gain: float32 [768], P('tensor'), may hold values from 0.25 to 1.75
- first_shift: float32 [768], P('tensor'), may hold values from -1.75 to 1.75
- up_weight: bfloat16 [768, 3072], P(None, 'tensor'), may hold values from -0.21875 to 0.21875
- up_bias: float32 [3072], P('tensor'), may hold values from -1.75 to 1.75
- down_weight: bfloat16 [3072, 768], P('tensor'), may hold values from -0.109375 to 0.109375
- down_bias: float32 [768], P('tensor'), may hold values from -1.75 to 1.75
- second_gain: float32 [768], P('tensor'), may hold values from 0.25 to 1.75
- second_shift: float32 [768], P('tensor'), may hold values from -1.75 to 1.75
- pool_weight: bfloat16 [768, 768], P('tensor'), may hold values from -0.21875 to 0.21875
- pool_bias: float32 [768], replicated, may hold values from -1.75 to 1.75
- log_temp: float32 [1], replicated, may hold values from -4.2 to -3.6
- segments: int32 [32, 1024], P('dp'), may hold values from 0 to 15, never falling along the last dimension, each value on 1 to 256 neighbouring positions
- cls_pos: int32 [32, 8], P('dp'), may hold values from 0 to 1023
- pair_index: int32 [256], P('dp'), may hold values from 0 to 255, each once
- attn_keep: int32 [32768, 768], P('dp', 'tensor'), may hold values 0 or 1
- ffn_keep: int32 [32768, 768], P('dp', 'tensor'), may hold values 0 or 1
- grad_out: bfloat16 [32768, 768], P('dp', 'tensor'), may hold values from -6 to 6
Outputs:
- layer_out: bfloat16 [32768, 768], P('dp', 'tensor')
- loss: float32 [1], replicated
- grad_tokens: float32 [32768, 768], P('dp', 'tensor')
- grad_qkv_weight: float32 [3, 768, 768], P(None, None, 'tensor')
- grad_qv_bias: float32 [2, 768], P(None, 'tensor')
- grad_out_weight: float32 [768, 768], P('tensor')
- grad_out_bias: float32 [768], P('tensor')
- grad_first_gain: float32 [768], P('tensor')
- grad_first_shift: float32 [768], P('tensor')
- grad_up_weight: float32 [768, 3072], P(None, 'tensor')
- grad_up_bias: float32 [3072], P('tensor')
- grad_down_weight: float32 [3072, 768], P('tensor')
- grad_down_bias: float32 [768], P('tensor')
- grad_second_gain: float32 [768], P('tensor')
- grad_second_shift: float32 [768], P('tensor')
- grad_pool_weight: float32 [768, 768], P('tensor')
- grad_pool_bias: float32 [768], replicated
- grad_log_temp: float32 [1], replicated
The draws below stay inside these ranges and needn't reach their ends.
Inputs may be any that keep to these rules, and one draw needn't show every extreme that they name: `segments`: segment numbers never fall along a packed row; a segment holds 1 to 256 positions. `pair_index`: every pooled row is named by exactly one row.
All inputs are finite; a program needn't handle non-finite values. No bound on the sum of `attn_keep` or of `ffn_keep` on one device may be relied on, other than what follows from the above.
Results may differ from the reference program's by a relative error of at most 0.015.
Values may be sent and summed in bfloat16 or wider, within the bound.
No kernel may reach another device: no remote copies, remote signals or barrier semaphores. Data moves between devices by JAX's collectives and lax.ppermute only.
A program may use at most 192 MiB of HBM per device.

```python
import math
import jax
import jax.numpy as jnp
import numpy as np
from jax import lax

D = 768
HEADS = 12
HEAD_DIM = 64
FF = 3072
LEN = 1024
CLS_ROW = 8
SEG_COUNT = 16
NROWS = 32
TOKENS = 32768
BATCH = 256


def place_ends(entries, rng, smallest, high):
    longest = entries.shape.index(max(entries.shape))
    spots = []
    for shift in (0, 1):
        where = [jax.random.randint(jax.random.fold_in(rng, axis), (), 0, length) for axis, length in enumerate(entries.shape)]
        where[longest] = (where[longest] + shift) % entries.shape[longest]
        spots.append(tuple(where))
    return entries.at[spots[0]].set(smallest).at[spots[1]].set(high)


def block_scale(own_key, extent, split, smallest, top_value):
    gain = 1.0
    for position, shards_of in split:
        draws = jax.random.uniform(jax.random.fold_in(jax.random.fold_in(own_key, 6), position), (shards_of,), jnp.float32, smallest / len(split), top_value / len(split))
        gain = gain * jnp.repeat(jnp.exp(draws), extent[position] // shards_of).reshape((-1,) + (1,) * (len(extent) - 1 - position))
    return gain


def profile(number_of, total, most, slope):
    loads = [(1 << 20) // math.isqrt(grade ** slope) + 1 for grade in range(2, number_of + 1)]
    spare, holding = total - most - (number_of - 1), [1] * (number_of - 1)
    while spare > 0:
        movable = [i for i in range(number_of - 1) if holding[i] < most]
        mass, remaining = sum([loads[i] for i in movable]), spare
        for i in movable:
            more = min(most - holding[i], max(1, remaining * loads[i] // mass), spare)
            holding[i] = holding[i] + more
            spare = spare - more
    return np.array([most] + holding)


def uneven_parts(own_key, count, total, most, lean):
    if count == 2:
        one = jax.random.randint(own_key, (), max(1, total - most), min(most, total - 1) + 1)
        return jnp.stack([one, total - one])
    tallies = jnp.asarray(profile(count, total, most, lean), jnp.int32)
    twos = (count - 1) // 2
    giver, sink = tallies[1:1 + 2 * twos:2], tallies[2:2 + 2 * twos:2]
    slack = jnp.minimum(giver - 1, most - sink)
    passed = jax.random.randint(jax.random.fold_in(own_key, 1), (twos,), 0, 1 << 20) % (slack + 1)
    tallies = tallies.at[1:1 + 2 * twos:2].set(giver - passed).at[2:2 + 2 * twos:2].set(sink + passed)
    return tallies[jax.random.permutation(jax.random.fold_in(own_key, 2), count)]


def centred(stream_key, shape, width, most, shards=(), held_as=jnp.bfloat16):
    values = width * jax.random.normal(stream_key, shape, jnp.float32)
    if shards:
        values = values * block_scale(stream_key, shape, shards, -0.22, 0.18)
    return jnp.clip(values, -most, most).astype(held_as)


def setup_inputs(seed: int = 0) -> dict:
    streams_of = jax.random.split(jax.random.key(seed), 23)
    return {
        "tokens": centred(streams_of[0], (TOKENS, D), 1.0, 6.0, ((0, 16), (1, 2))),
        "qkv_weight": centred(streams_of[1], (3, D, D), D ** -0.5, 0.21875, ((2, 2),)),
        "qv_bias": centred(streams_of[2], (2, D), 0.3, 1.75, ((1, 2),), jnp.float32),
        "out_weight": centred(streams_of[3], (D, D), (D // 16) ** -0.5, 0.875, ((0, 2),)),
        "out_bias": centred(streams_of[4], (D,), 0.3, 1.75, ((0, 2),), jnp.float32),
        "first_gain": jnp.clip(1.0 + 0.15 * jax.random.normal(streams_of[5], (D,), jnp.float32), 0.25, 1.75),
        "first_shift": centred(streams_of[6], (D,), 0.3, 1.75, ((0, 2),), jnp.float32),
        "up_weight": centred(streams_of[7], (D, FF), D ** -0.5, 0.21875, ((1, 2),)),
        "up_bias": centred(streams_of[8], (FF,), 0.3, 1.75, ((0, 2),), jnp.float32),
        "down_weight": centred(streams_of[9], (FF, D), FF ** -0.5, 0.109375, ((0, 2),)),
        "down_bias": centred(streams_of[10], (D,), 0.3, 1.75, ((0, 2),), jnp.float32),
        "second_gain": jnp.clip(1.0 + 0.15 * jax.random.normal(streams_of[11], (D,), jnp.float32), 0.25, 1.75),
        "second_shift": centred(streams_of[12], (D,), 0.3, 1.75, ((0, 2),), jnp.float32),
        "pool_weight": centred(streams_of[13], (D, D), D ** -0.5, 0.21875, ((0, 2),)),
        "pool_bias": centred(streams_of[14], (D,), 0.3, 1.75, (), jnp.float32),
        "log_temp": jnp.clip(jax.random.uniform(streams_of[15], (1,), jnp.float32, -4.2, -3.6), -4.2, -3.6),
        "segments": jax.vmap(lambda own: jnp.searchsorted(jnp.cumsum(uneven_parts(own, SEG_COUNT, LEN, LEN // 4, 1)), jnp.arange(LEN), side="right"))(jax.random.split(streams_of[16], NROWS)).reshape((NROWS, LEN)).astype(jnp.int32),
        "cls_pos": place_ends(jax.random.randint(streams_of[17], (NROWS, CLS_ROW), 0, LEN), jax.random.fold_in(streams_of[17], 1), 0, LEN - 1).astype(jnp.int32),
        "pair_index": jax.random.permutation(streams_of[18], BATCH).astype(jnp.int32),
        "attn_keep": place_ends((jax.random.randint(streams_of[19], (TOKENS, D), 0, 10) < 9).astype(jnp.int32), jax.random.fold_in(streams_of[19], 1), 0, 1),
        "ffn_keep": place_ends((jax.random.randint(streams_of[20], (TOKENS, D), 0, 10) < 9).astype(jnp.int32), jax.random.fold_in(streams_of[20], 1), 0, 1),
        "grad_out": centred(streams_of[21], (TOKENS, D), 1.0, 6.0, ((0, 16), (1, 2))),
    }


@jax.custom_vjp
def low(v):
    return lax.optimization_barrier(v.astype(jnp.bfloat16)).astype(jnp.float32)

@jax.custom_vjp
def low_back(v):
    return v

def low_keep(v):
    return (low(v), None)

def low_pass(kept, grad):
    return (grad,)

def back_keep(v):
    return (v, None)

def back_low(kept, grad):
    return (low(grad),)
low.defvjp(low_keep, low_pass)
low_back.defvjp(back_keep, back_low)
highest = lax.Precision.HIGHEST

def round_both(incoming):
    return low(low_back(incoming))

def layer_norm(incoming, norm_gain, norm_shift):
    center = incoming - lax.optimization_barrier(jnp.mean(incoming, axis=-1, keepdims=True))
    spread = lax.optimization_barrier(jnp.mean(center * center, axis=-1, keepdims=True))
    return center * lax.rsqrt(spread + 1e-06) * norm_gain + norm_shift

def attend_group(pieces):
    queries, key_heads, values, labels = pieces
    scores = jnp.einsum('gqhe,gkhe->ghqk', queries, key_heads, precision=highest) * HEAD_DIM ** (-0.5)
    scores = low_back(scores)
    allowed = labels[:, :, None] == labels[:, None, :]
    scores = jnp.where(allowed[:, None], scores, -1e+30)
    row_top = lax.optimization_barrier(jnp.max(scores, axis=-1, keepdims=True))
    row_expo = jnp.exp(scores - row_top)
    attn_probs = low(row_expo / lax.optimization_barrier(jnp.sum(row_expo, axis=-1, keepdims=True)))
    return jnp.einsum('ghqk,gkhe->gqhe', attn_probs, values, precision=highest)

def forward(params, tokens, labels, cls_flat, pair_index, attn_keep, ffn_keep):
    qkv_weight, qv_bias, out_weight, out_bias, first_gain, first_shift, up_weight, up_bias, down_weight, down_bias, second_gain, second_shift, pool_weight, pool_bias, log_temp = params
    width_all = tokens.shape[1]
    projected = jnp.einsum('td,cde->cte', tokens, qkv_weight, precision=highest)
    bias_rows = jnp.stack([qv_bias[0], jnp.zeros_like(qv_bias[0]), qv_bias[1]])
    projected = round_both(projected + bias_rows[:, None, :])
    rows_all = labels.shape[0]
    group_size = math.gcd(rows_all, max(1, 4096 // LEN))
    shaped = projected.reshape(3, rows_all // group_size, group_size, LEN, HEADS, HEAD_DIM)
    grouped = labels.reshape(rows_all // group_size, group_size, LEN)
    context = lax.map(jax.checkpoint(attend_group), (shaped[0], shaped[1], shaped[2], grouped))
    context = round_both(context.reshape(tokens.shape[0], width_all))
    branch = low_back(jnp.dot(context, out_weight, precision=highest) + out_bias)
    residual = tokens + branch * attn_keep / 0.9
    hidden = layer_norm(residual, first_gain, first_shift)
    upper_pre = low_back(jnp.dot(low(hidden), up_weight, precision=highest) + up_bias)
    active = low(jax.nn.gelu(upper_pre, approximate=False))
    ffn_out = low_back(jnp.dot(active, down_weight, precision=highest) + down_bias)
    mixed_sum = hidden + ffn_out * ffn_keep / 0.9
    layer_value = layer_norm(mixed_sum, second_gain, second_shift)
    pooled = layer_value[cls_flat]
    pool_pre = low_back(jnp.dot(low(pooled), pool_weight, precision=highest) + pool_bias)
    squash = low(jnp.tanh(pool_pre))
    unit_rows = squash * lax.rsqrt(lax.optimization_barrier(jnp.sum(squash * squash, axis=-1, keepdims=True)) + 1e-06)
    logits = jnp.dot(unit_rows, unit_rows.T, precision=highest) * jnp.exp(-log_temp[0])
    columns = jnp.arange(logits.shape[0], dtype=jnp.int32)
    masked = jnp.where(columns[:, None] == columns[None, :], -1e+30, logits)
    row_top = lax.optimization_barrier(jnp.max(masked, axis=-1, keepdims=True))
    log_total = row_top[:, 0] + jnp.log(lax.optimization_barrier(jnp.sum(jnp.exp(masked - row_top), axis=-1)))
    positive = lax.optimization_barrier(jnp.sum(jnp.where(columns[None, :] == pair_index[:, None], logits, 0.0), axis=-1))
    return (layer_value, jnp.sum(log_total - positive))

def reference(tokens, qkv_weight, qv_bias, out_weight, out_bias, first_gain, first_shift, up_weight, up_bias, down_weight, down_bias, second_gain, second_shift, pool_weight, pool_bias, log_temp, segments, cls_pos, pair_index, attn_keep, ffn_keep, grad_out):
    params = tuple((item.astype(jnp.float32) for item in (qkv_weight, qv_bias, out_weight, out_bias, first_gain, first_shift, up_weight, up_bias, down_weight, down_bias, second_gain, second_shift, pool_weight, pool_bias, log_temp)))
    tokens_f = tokens.astype(jnp.float32)
    rows_all = segments.shape[0]
    cls_flat = (jnp.arange(rows_all, dtype=jnp.int32)[:, None] * LEN + cls_pos).reshape(-1).astype(jnp.int32)
    attn_float = attn_keep.astype(jnp.float32)
    ffn_float = ffn_keep.astype(jnp.float32)

    def objective(param_list, token_list):
        return forward(param_list, token_list, segments, cls_flat, pair_index, attn_float, ffn_float)
    (layer_value, loss_sum), pullback = jax.vjp(objective, params, tokens_f)
    grad_params, grad_tokens = pullback((grad_out.astype(jnp.float32), jnp.ones_like(loss_sum)))
    grad_qkv, grad_qv, grad_outw, grad_outb, grad_g1, grad_s1, grad_upw, grad_upb, grad_downw, grad_downb, grad_g2, grad_s2, grad_poolw, grad_poolb, grad_temp = grad_params
    loss_mean = (loss_sum / BATCH).reshape(1)
    return (layer_value.astype(jnp.bfloat16), loss_mean, grad_tokens, grad_qkv, grad_qv, grad_outw, grad_outb, grad_g1, grad_s1, grad_upw, grad_upb, grad_downw, grad_downb, grad_g2, grad_s2, grad_poolw, grad_poolb, grad_temp)
```

```python
import functools
import jax
import jax.numpy as jnp
from jax import lax
from jax.experimental import pallas as pl
from jax.experimental.pallas import tpu as pltpu
from jax.sharding import PartitionSpec as P

D = 768
HEAD_DIM = 64
PAIR = 2 * HEAD_DIM
BLOCK = 256
QROWS = 128
WIDE = QROWS + 512
NEAR = QROWS + 256
SWAP = [(0, 1), (1, 0)]
highest = lax.Precision.HIGHEST
f32 = jnp.float32
bf16 = jnp.bfloat16


def dot_nt(a, b, **kw):
    return lax.dot_general(a, b, (((1,), (1,)), ((), ())), preferred_element_type=f32, **kw)


def dot_tn(a, b):
    return lax.dot_general(a, b, (((0,), (0,)), ((), ())), preferred_element_type=f32)


def dot_nn(a, b):
    return jnp.dot(a, b, preferred_element_type=f32)


ORDER = []

MICROS = {
    "their_rows": 2, "vectors": 1, "qkv": 5, "pooled": 9, "attend": 11, "ffn": 25, "contrast": 6, "down_back": 9,
    "down_own": 3.5, "up_back": 10, "up_own": 10, "out_back": 9, "attend_back": 21, "qkv_last": 4,
    "tokens_back": 5, "last_quarters": 2, "stage": 1, "up_end": 3, "last_end": 3, "down_end": 3,
}


def norm(v):
    center = v - jnp.mean(v, axis=-1, keepdims=True)
    inv = lax.rsqrt(jnp.mean(center * center, axis=-1, keepdims=True) + 1e-06)
    return center * inv, inv


def norm_back(upstream, unit, inv, gain):
    scaled = upstream * gain
    return inv * (
        scaled
        - jnp.mean(scaled, axis=-1, keepdims=True)
        - unit * jnp.mean(scaled * unit, axis=-1, keepdims=True)
    )


def gelu_both(x):
    phi = 0.5 * (1.0 + lax.erf(x * (0.5 ** 0.5)))
    bell = jnp.exp(-0.5 * x * x) * 0.3989422804014327
    return x * phi, phi + x * bell


def lanes_of(me, half):
    return pl.ds(pl.multiple_of(me * half, 128), half)


def call(kernel, name, grid, scalars, ins, outs, scratch=(), vmem=26, after=(), aliases=None):
    after = [*after, *ORDER[-1:]]
    n_scalars, n_ins, n_after = len(scalars), len(ins), len(after)

    def body(*refs):
        cut = n_scalars + n_ins
        kernel(*refs[:cut], *refs[cut + n_after :])

    def spec(shape, block, index):
        if block is None:
            zeros = (0,) * len(shape)
            return pl.BlockSpec(shape, lambda *a: zeros)
        return pl.BlockSpec(block, index)

    arrays = [a if b is None else pltpu.with_memory_space_constraint(a, pltpu.HBM) for a, b, _ in ins]
    result = pl.pallas_call(
        body,
        grid_spec=pltpu.PrefetchScalarGridSpec(
            num_scalar_prefetch=len(scalars),
            grid=grid,
            in_specs=[spec(a.shape, b, i) for a, b, i in ins]
            + [pl.BlockSpec(memory_space=pl.ANY)] * n_after,
            out_specs=[spec(s, b, i) for s, _, b, i in outs],
            scratch_shapes=list(scratch),
        ),
        out_shape=[jax.ShapeDtypeStruct(s, d) for s, d, _, _ in outs],
        compiler_params=pltpu.CompilerParams(vmem_limit_bytes=vmem << 20),
        cost_estimate=pl.CostEstimate(flops=int(MICROS[name] * 1.15e9), bytes_accessed=1000, transcendentals=0),
        input_output_aliases={n_scalars + i: o for i, o in (aliases or {}).items()},
        name=name,
    )(*scalars, *arrays, *after)
    ORDER.append(min(result, key=lambda r: r.size))
    return result


def put_halves(buf, me, mine, theirs):
    half = mine.shape[1]
    buf[:, lanes_of(me, half)] = mine.astype(buf.dtype)
    buf[:, lanes_of(1 - me, half)] = theirs.astype(buf.dtype)


def rows_kernel(me_ref, *refs):
    for i, o in zip(refs[: len(refs) // 2], refs[len(refs) // 2 :]):
        o[...] = i[...].astype(bf16)


def their_rows(me, arrays, length, after=()):
    half = arrays[0].shape[1]
    steps = length // 512
    return call(
        rows_kernel, "their_rows", (steps,), [me],
        [(a, (512, half), lambda i, m: ((1 - m[0]) * steps + i, 0)) for a in arrays],
        [((length, half), bf16, (512, half), lambda i, m: (i, 0))] * len(arrays),
        after=after,
    )


def vectors_kernel(units, me_ref, mine, theirs, qv_ref, up_ref, feats_ref):
    half = qv_ref.shape[1] // 2
    feats_ref[...] = jnp.zeros_like(feats_ref)
    for side, vec in enumerate((mine, theirs)):
        for row in range(2):
            qv_ref[row : row + 1, side * half : side * half + half] = vec[:, row * half : row * half + half]
        up_ref[:, side * units : side * units + units] = vec[:, 2 * half : 2 * half + units]
        spot = lanes_of(me_ref[0] if side == 0 else 1 - me_ref[0], half)
        for row in range(6):
            low = 2 * half + units + row * half
            feats_ref[row : row + 1, spot] = vec[:, low : low + half]


def vectors(me, mine, theirs, units, half):
    return call(
        functools.partial(vectors_kernel, units), "vectors", (1,), [me],
        [(mine, None, None), (theirs, None, None)],
        [((2, 2 * half), f32, None, None), ((1, 2 * units), f32, None, None), ((8, 2 * half), f32, None, None)],
    )


def qkv_kernel(me_ref, mine, theirs, w_here, w_there, bias, x_ref, q_ref, k_ref, v_ref):
    put_halves(x_ref, me_ref[0], mine[...], theirs[...])
    half = mine.shape[1]
    for c, out in enumerate((q_ref, k_ref, v_ref)):
        for side, w in enumerate((w_here, w_there)):
            cols = slice(side * half, side * half + half)
            y = dot_nn(x_ref[...], w[c])
            if c != 1:
                y = y + bias[c // 2 : c // 2 + 1, cols]
            out[:, cols] = y.astype(bf16)


def project(me, tokens, x_there, w_here, w_there, bias, length):
    half = tokens.shape[1]
    rows = 512
    steps = length // rows
    band = (rows, 2 * half)
    return call(
        qkv_kernel, "qkv", (steps,), [me],
        [
            (tokens, (rows, half), lambda i, m: (m[0] * steps + i, 0)),
            (x_there, (rows, half), lambda i, m: (i, 0)),
            (w_here, None, None),
            (w_there, None, None),
            (bias, None, None),
        ],
        [((length, 2 * half), bf16, band, lambda i, m: (i, 0))] * 4,
    )


def window_paths(step, length, seg_ref, run):
    first = step * QROWS
    near = pl.multiple_of(jnp.clip(first - 128, 0, length - NEAR), 128)
    left = seg_ref[jnp.maximum(near - 1, 0)] == seg_ref[first]
    right = seg_ref[jnp.minimum(near + NEAR, length - 1)] == seg_ref[first + QROWS - 1]
    spills = jnp.logical_or(
        jnp.logical_and(near > 0, left), jnp.logical_and(near + NEAR < length, right)
    )
    far = pl.multiple_of(jnp.clip(first - 256, 0, length - WIDE), 128)

    @pl.when(jnp.logical_not(spills))
    def _():
        run(NEAR, near)

    @pl.when(spills)
    def _():
        run(WIDE, far)


def fill_bias(bias_ref, col_ref, row_ref, width, start):
    bias = jnp.where(col_ref[pl.ds(start, width), :] == row_ref[...], 0.0, -1e30)
    for n in range(bias_ref.shape[1] // QROWS):
        bias_ref[0:width, n * QROWS : (n + 1) * QROWS] = bias


def head_mask(h):
    lane = lax.broadcasted_iota(jnp.int32, (1, PAIR), 1)
    return (lane // HEAD_DIM == h).astype(bf16)


def attend_kernel(length, pairs, seg_ref, col_ref, row_ref, q_ref, k_ref, v_ref, ctx_ref, lse_ref, bias_ref):
    def run(width, start):
        fill_bias(bias_ref, col_ref, row_ref, width, start)
        rows = pl.ds(start, width)
        for j in range(pairs):
            lanes = slice(j * PAIR, j * PAIR + PAIR)
            q2 = q_ref[:, lanes] * bf16(HEAD_DIM ** (-0.5))
            keys = k_ref[rows, lanes]
            values = v_ref[rows, lanes]
            parts = []
            for h in range(2):
                scores = dot_nt(keys, q2 * head_mask(h)) + bias_ref[0:width, :]
                top = jnp.max(scores, axis=0, keepdims=True)
                expo = jnp.exp(scores - top)
                total = jnp.sum(expo, axis=0, keepdims=True)
                out = dot_tn(values, expo.astype(bf16))[h * HEAD_DIM : (h + 1) * HEAD_DIM]
                parts.append(out * (1.0 / total))
                lse_ref[8 * h + j : 8 * h + j + 1, :] = top + jnp.log(total)
            ctx_ref[:, lanes] = jnp.concatenate(parts, axis=0).T.astype(bf16)

    window_paths(pl.program_id(0), length, seg_ref, run)


def attend(seg, col, q, k, v, after):
    length, width = q.shape
    band = lambda i, s: (i, 0)
    block = (QROWS, width)
    return call(
        functools.partial(attend_kernel, length, width // PAIR), "attend", (length // QROWS,),
        [seg.reshape(length)],
        [
            (col, None, None),
            (seg.reshape(1, length), (1, QROWS), lambda i, s: (0, i)),
            (q, block, band),
            (k, None, None),
            (v, None, None),
        ],
        [
            ((length, width), bf16, block, band),
            ((16, length), f32, (16, QROWS), lambda i, s: (0, i)),
        ],
        [pltpu.VMEM((WIDE, QROWS), f32)],
        after=after,
    )


def attend_back_kernel(
    length, chosen, seg_ref, col_ref, row_ref, q_ref, k_ref, v_ref, do_ref, lse_ref, delta_ref,
    dq_ref, dk_ref, dv_ref, bias_ref, dk_acc, dv_acc,
):
    step = pl.program_id(0)

    @pl.when(step == 0)
    def _():
        dk_acc[...] = jnp.zeros_like(dk_acc)
        dv_acc[...] = jnp.zeros_like(dv_acc)

    def both(ref, j):
        return jnp.concatenate([ref[j : j + 1, :], ref[8 + j : 9 + j, :]], axis=1)

    def run(width, start):
        fill_bias(bias_ref, col_ref, row_ref, width, start)
        rows = pl.ds(start, width)
        for n, j in enumerate(chosen):
            lanes = slice(j * PAIR, j * PAIR + PAIR)
            slot = slice(n * PAIR, n * PAIR + PAIR)
            q2 = q_ref[:, lanes] * bf16(HEAD_DIM ** (-0.5))
            do2 = do_ref[:, lanes]
            keys = k_ref[rows, lanes]
            values = v_ref[rows, lanes]
            queries = jnp.concatenate([q2 * head_mask(0), q2 * head_mask(1)], axis=0)
            grads = jnp.concatenate([do2 * head_mask(0), do2 * head_mask(1)], axis=0)
            scores = dot_nt(keys, queries) + bias_ref[0:width, :]
            probs = jnp.exp(scores - both(lse_ref, j))
            grad_probs = dot_nt(values, grads)
            grad_scores = (probs * (grad_probs - both(delta_ref, j))).astype(bf16)
            dv_acc[rows, slot] += dot_nn(probs.astype(bf16), grads)
            dk_acc[rows, slot] += dot_nn(grad_scores, queries)
            dq = dot_tn(keys, grad_scores)
            dq = jnp.concatenate([dq[:HEAD_DIM, :QROWS], dq[HEAD_DIM:, QROWS:]], axis=0).T
            dq_ref[:, slot] = (dq * (HEAD_DIM ** (-0.5))).astype(bf16)

    window_paths(step, length, seg_ref, run)

    @pl.when(step == length // QROWS - 1)
    def _():
        dk_ref[...] = dk_acc[...].astype(bf16)
        dv_ref[...] = dv_acc[...].astype(bf16)


def attend_back(seg, col, q, k, v, grad_ctx, lse, delta, chosen, after):
    length, width = q.shape
    cols = len(chosen) * PAIR
    block = (QROWS, width)
    band = lambda i, s: (i, 0)
    flat = lambda i, s: (0, i)
    whole = ((length, cols), bf16, None, None)
    return call(
        functools.partial(attend_back_kernel, length, chosen), "attend_back", (length // QROWS,),
        [seg.reshape(length)],
        [
            (col, None, None),
            (seg.reshape(1, length), (1, QROWS), flat),
            (q, block, band),
            (k, None, None),
            (v, None, None),
            (grad_ctx, block, band),
            (lse, (16, QROWS), flat),
            (delta, (16, QROWS), flat),
        ],
        [((length, cols), bf16, (QROWS, cols), band), whole, whole],
        [
            pltpu.VMEM((WIDE, 2 * QROWS), f32),
            pltpu.VMEM((length, cols), f32),
            pltpu.VMEM((length, cols), f32),
        ],
        after=after,
    )


def pooled_kernel(
    length, pairs, me_ref, seg_ref, cls_ref, pair_ref, row_ref, q_ref, k_ref, v_ref, x_ref, keep1_mine, keep1_theirs,
    keep2_mine, keep2_theirs, ow_here, ow_there, uw_here, uw_there, dw_here, dw_there, up_b, feats,
    out_ref, keep1, keep2,
):
    count = cls_ref.shape[0]
    sub = lax.broadcasted_iota(jnp.int32, (16, length), 0)
    lane = lax.broadcasted_iota(jnp.int32, (16, length), 1)
    spot = jnp.zeros((16, length), jnp.int32)
    label = jnp.zeros((16, length), jnp.int32)
    for c in range(count):
        spot = jnp.where(sub == c, cls_ref[c], spot)
        label = jnp.where(sub == c, seg_ref[cls_ref[c]], label)
    pick = (lane == spot).astype(bf16)
    put_halves(keep1, me_ref[0], dot_nn(pick, keep1_mine[...].astype(bf16)), dot_nn(pick, keep1_theirs[...]))
    put_halves(keep2, me_ref[0], dot_nn(pick, keep2_mine[...].astype(bf16)), dot_nn(pick, keep2_theirs[...]))
    queries = dot_nn(pick, q_ref[...]).astype(bf16) * bf16(HEAD_DIM ** (-0.5))
    x = dot_nn(pick, x_ref[...])
    bias = jnp.where(label == row_ref[...], 0.0, -1e30)
    bias = jnp.concatenate([bias, bias], axis=0)
    head_lane = lax.broadcasted_iota(jnp.int32, (16, PAIR), 1) < HEAD_DIM
    parts = []
    for j in range(pairs):
        lanes = slice(j * PAIR, j * PAIR + PAIR)
        two = jnp.concatenate([queries[:, lanes] * head_mask(0), queries[:, lanes] * head_mask(1)], axis=0)
        scores = dot_nt(two, k_ref[:, lanes]) + bias
        expo = jnp.exp(scores - jnp.max(scores, axis=-1, keepdims=True))
        out = dot_nn(expo.astype(bf16), v_ref[:, lanes]) / jnp.sum(expo, axis=-1, keepdims=True)
        parts.append(jnp.where(head_lane, out[:16], out[16:]))
    ctx = jnp.concatenate(parts, axis=1).astype(bf16)
    half = ow_here.shape[0]
    branch = dot_nn(ctx[:, :half], ow_here[...]) + dot_nn(ctx[:, half:], ow_there[...]) + feats[0:1, :]
    residual = x + branch * (keep1[...] * (1 / 0.9))
    hidden = norm(residual)[0] * feats[1:2, :] + feats[2:3, :]
    low = hidden.astype(bf16)
    units = uw_here.shape[1]
    ffn = jnp.zeros((16, x.shape[1]), f32)
    for side, (up, down) in enumerate(((uw_here, dw_here), (uw_there, dw_there))):
        pre = dot_nn(low, up[...]) + up_b[:, side * units : (side + 1) * units]
        ffn = ffn + dot_nn(gelu_both(pre)[0].astype(bf16), down[...])
    mixed = hidden + (ffn + feats[3:4, :]) * (keep2[...] * (1 / 0.9))
    value = norm(mixed)[0] * feats[4:5, :] + feats[5:6, :]
    out_row = lax.broadcasted_iota(jnp.int32, (16, 128), 0)
    out_lane = lax.broadcasted_iota(jnp.int32, (16, 128), 1)
    extra = jnp.zeros((16, 128), jnp.int32)
    for c in range(count):
        number = pair_ref[me_ref[0] * count + c]
        extra = jnp.where((out_lane == c) & (out_row == count), number // 64, extra)
        extra = jnp.where((out_lane == c) & (out_row == count + 1), number % 64, extra)
    extra = jnp.concatenate([extra.astype(f32), jnp.zeros((16, x.shape[1] - 128), f32)], axis=1)
    is_row = lax.broadcasted_iota(jnp.int32, value.shape, 0) < count
    out_ref[...] = jnp.where(is_row, value, extra).astype(bf16)


def pooled_rows(me, seg, cls, pair_index, q, k, v, x, keep1, keep2, weights, up_b, feats):
    length, width = q.shape
    half = width // 2
    part = lambda a: (a, (length, half), lambda i, m, s, c, p: (m[0], 0))
    whole = lambda a: (a, None, None)
    return call(
        functools.partial(pooled_kernel, length, width // PAIR), "pooled", (1,), [me, seg.reshape(length), cls, pair_index],
        [
            whole(seg.reshape(1, length)), whole(q), whole(k), whole(v), whole(x),
            part(keep1[0]), whole(keep1[1]), part(keep2[0]), whole(keep2[1]),
            *[whole(w) for w in weights], whole(up_b), whole(feats),
        ],
        [((16, width), bf16, None, None)],
        [pltpu.VMEM((16, width), f32), pltpu.VMEM((16, width), f32)],
    )[0]


UNITS = 512
FROWS = 512


def sides(sides_count, step, here_first, run_here, run_there):
    low, high = (run_here, run_there) if here_first else (run_there, run_here)

    @pl.when(step < sides_count)
    def _():
        low()

    @pl.when(step >= sides_count)
    def _():
        high()


def ffn_kernel(
    count, me_ref, ctx_ref, x_ref, ow_here, ow_there, keep1_mine, keep1_theirs, uw_here, uw_there, dw_here,
    dw_there, up_b, feats, keep_mine, keep_theirs, res_ref, low_ref, act_ref, slope_ref, mixed_ref, mine_ref,
    theirs_ref, keep, value_buf,
):
    step = pl.program_id(0)
    length = low_ref.shape[0]

    @pl.when(step == 0)
    def _():
        mixed_ref[...] = jnp.zeros_like(mixed_ref)
        side = ow_here.shape[0]
        for r in range(length // BLOCK):
            rows = slice(r * BLOCK, (r + 1) * BLOCK)
            put_halves(keep, me_ref[0], keep1_mine[rows, :].astype(f32), keep1_theirs[rows, :])
            branch = dot_nn(ctx_ref[rows, :side], ow_here[...]) + dot_nn(ctx_ref[rows, side:], ow_there[...])
            residual = x_ref[rows, :].astype(f32) + (branch + feats[0:1, :]) * (keep[...] * (1 / 0.9))
            res_ref[rows, :] = residual
            low_ref[rows, :] = (norm(residual)[0] * feats[1:2, :] + feats[2:3, :]).astype(bf16)

    def run(up, down):
        def go():
            for r in range(length // FROWS):
                rows = slice(r * FROWS, (r + 1) * FROWS)
                pre = dot_nn(low_ref[rows, :], up[...]) + up_b[...]
                value, slope = gelu_both(pre)
                value = value.astype(bf16)
                act_ref[rows, :] = value
                slope_ref[rows, :] = slope.astype(bf16)
                mixed_ref[rows, :] += dot_nn(value, down[...])

        return go

    sides(count, step, True, run(uw_here, dw_here), run(uw_there, dw_there))

    @pl.when(step == 2 * count - 1)
    def _():
        half = mine_ref.shape[1]
        me = me_ref[0]
        for r in range(length // BLOCK):
            rows = slice(r * BLOCK, (r + 1) * BLOCK)
            put_halves(keep, me, keep_mine[rows, :].astype(f32), keep_theirs[rows, :])
            hidden = norm(res_ref[rows, :])[0] * feats[1:2, :] + feats[2:3, :]
            mixed = hidden + (mixed_ref[rows, :] + feats[3:4, :]) * (keep[...] * (1 / 0.9))
            mixed_ref[rows, :] = mixed
            value_buf[...] = (norm(mixed)[0] * feats[4:5, :] + feats[5:6, :]).astype(bf16)
            mine_ref[rows, :] = value_buf[:, lanes_of(me, half)]
            theirs_ref[rows, :] = value_buf[:, lanes_of(1 - me, half)]


def feed_forward(me, ctx, x, ow_here, ow_there, keep1, uw_here, uw_there, dw_here, dw_there, up_b, feats, keep):
    length, width = x.shape
    half = width // 2
    count = uw_here.shape[1] // UNITS
    units = 2 * uw_here.shape[1]
    first = lambda i: jnp.minimum(i, count - 1)
    second = lambda i: jnp.maximum(i - count, 0)
    return call(
        functools.partial(ffn_kernel, count), "ffn", (2 * count,), [me],
        [
            (ctx, None, None),
            (x, None, None),
            (ow_here, None, None),
            (ow_there, None, None),
            (keep1[0], (length, half), lambda i, m: (m[0], 0)),
            (keep1[1], None, None),
            (uw_here, (width, UNITS), lambda i, m: (0, first(i))),
            (uw_there, (width, UNITS), lambda i, m: (0, second(i))),
            (dw_here, (UNITS, width), lambda i, m: (first(i), 0)),
            (dw_there, (UNITS, width), lambda i, m: (second(i), 0)),
            (up_b, (1, UNITS), lambda i, m: (0, i)),
            (feats, None, None),
            (keep[0], (length, half), lambda i, m: (m[0], 0)),
            (keep[1], None, None),
        ],
        [
            ((length, width), f32, None, None),
            ((length, width), bf16, None, None),
            ((length, units), bf16, (length, UNITS), lambda i, m: (0, i)),
            ((length, units), bf16, (length, UNITS), lambda i, m: (0, i)),
            ((length, width), f32, None, None),
            ((length, half), bf16, None, None),
            ((length, half), bf16, None, None),
        ],
        [pltpu.VMEM((BLOCK, width), f32), pltpu.VMEM((BLOCK, width), bf16)],
        vmem=36,
    )


def down_back_kernel(
    me_ref, cls_ref, mixed_ref, go_mine, go_theirs, pooled_ref, feats, keep_mine, keep_theirs, act_ref,
    g_ref, gm_ref, sums_ref, there_ref, buf, keep,
):
    length, width = mixed_ref.shape

    @pl.when(pl.program_id(0) == 0)
    def _():
        me = me_ref[0]
        put_halves(buf, me, go_mine[...].astype(f32), go_theirs[...])
        for c in range(cls_ref.shape[0]):
            spot = pl.ds(cls_ref[c], 1)
            buf[spot, :] = buf[spot, :] + pooled_ref[c : c + 1, :]
        gain_sum = jnp.zeros((1, width), f32)
        shift_sum = jnp.zeros((1, width), f32)
        bias_sum = jnp.zeros((1, width), f32)
        for r in range(length // BLOCK):
            rows = slice(r * BLOCK, (r + 1) * BLOCK)
            upstream = buf[rows, :]
            unit, inv = norm(mixed_ref[rows, :])
            back = norm_back(upstream, unit, inv, feats[4:5, :])
            gm_ref[rows, :] = back
            put_halves(keep, me, keep_mine[rows, :].astype(f32), keep_theirs[rows, :])
            g = (back * (keep[...] * (1 / 0.9))).astype(bf16)
            g_ref[rows, :] = g
            gain_sum = gain_sum + jnp.sum(upstream * unit, axis=0, keepdims=True)
            shift_sum = shift_sum + jnp.sum(upstream, axis=0, keepdims=True)
            bias_sum = bias_sum + jnp.sum(g.astype(f32), axis=0, keepdims=True)
        sums_ref[...] = jnp.concatenate(
            [bias_sum, gain_sum, shift_sum, jnp.zeros((5, width), f32)], axis=0
        )

    there_ref[...] = dot_tn(act_ref[...], g_ref[...]).astype(bf16)


def down_back(me, cls, mixed, go_arg, go_there, grad_pooled, feats, keep, act):
    length, width = mixed.shape
    half = width // 2
    units = act.shape[1] // 2
    count = units // UNITS
    part = lambda a: (a, (length, half), lambda i, m, c: (m[0], 0))
    return call(
        down_back_kernel, "down_back", (count,), [me, cls],
        [
            (mixed, None, None),
            part(go_arg),
            (go_there, None, None),
            (grad_pooled, None, None),
            (feats, None, None),
            part(keep[0]),
            (keep[1], None, None),
            (act, (length, UNITS), lambda i, m, c: (0, i + count)),
        ],
        [
            ((length, width), bf16, None, None),
            ((length, width), f32, None, None),
            ((8, width), f32, None, None),
            ((units, width), bf16, (UNITS, width), lambda i, m, c: (i, 0)),
        ],
        [pltpu.VMEM((length, width), f32), pltpu.VMEM((BLOCK, width), f32)],
    )


def down_own_kernel(place_ref, act_ref, g_ref, got_ref, o0, o1, o2, o3):
    grad = (dot_tn(act_ref[...], g_ref[...]) + got_ref[...].astype(f32)).astype(bf16)
    for m, out in enumerate((o0, o1, o2, o3)):
        @pl.when(pl.program_id(0) == place_ref[0] ^ m)
        def _():
            out[...] = grad


def down_own(spot, act, g, got):
    length, width = g.shape
    rows = got.shape[0] // 4
    return call(
        down_own_kernel, "down_own", (4,), [spot],
        [
            (act, (length, rows), lambda i, s: (0, i)),
            (g, None, None),
            (got, (rows, width), lambda i, s: (i, 0)),
        ],
        [((rows, width), bf16, None, None)] * 4,
    )


def up_back_kernel(
    own, spot_ref, low_ref, g_ref, slope_ref, up, down, *refs,
):
    if own:
        start_ref, got_ref, part_ref, bias_ref, *out_refs, grad_buf = refs
    else:
        part_ref, bias_ref, out_ref = refs
    step = pl.program_id(0)
    length, width = g_ref.shape

    @pl.when(step == 0)
    def _():
        part_ref[...] = start_ref[...] if own else jnp.zeros_like(part_ref)

    total = jnp.zeros((1, UNITS), f32)
    grads = []
    for r in range(length // FROWS):
        rows = slice(r * FROWS, (r + 1) * FROWS)
        gu = (dot_nt(g_ref[rows, :], down[...]) * slope_ref[rows, :].astype(f32)).astype(bf16)
        total = total + jnp.sum(gu.astype(f32), axis=0, keepdims=True)
        part_ref[rows, :] += dot_nt(gu, up[...])
        grads.append(gu)
    bias_ref[...] = total
    grad = dot_tn(low_ref[...], jnp.concatenate(grads, axis=0))
    if own:
        grad_buf[...] = (grad + got_ref[...].astype(f32)).astype(bf16)
        quarters_out(spot_ref[0], grad_buf, out_refs)
    else:
        out_ref[...] = grad.astype(bf16)


def up_back(spot, low, g, slope, up, down, own, start=None, got=None, after=()):
    length, width = g.shape
    units = up.shape[1]
    count = units // UNITS
    skip = 0 if own else count
    ins = [
        (low, None, None),
        (g, None, None),
        (slope, (length, UNITS), lambda i, s: (0, i + skip)),
        (up, (width, UNITS), lambda i, s: (0, i)),
        (down, (UNITS, width), lambda i, s: (i, 0)),
    ]
    rows = width // 4 if own else width
    outs = [
        ((length, width), f32, None, None),
        ((1, units), f32, (1, UNITS), lambda i, s: (0, i)),
    ] + [((rows, units), bf16, (rows, UNITS), lambda i, s: (0, i))] * (width // rows)
    scratch = []
    if own:
        scratch = [pltpu.VMEM((width, UNITS), bf16)]
        ins += [(start, None, None), (got, (width, UNITS), lambda i, s: (0, i))]
    return call(
        functools.partial(up_back_kernel, own), "up_own" if own else "up_back", (count,), [spot], ins, outs, scratch,
        after=after,
    )


def out_back_kernel(
    me_ref, gm_ref, part_ref, res_ref, ctx_ref, keep_mine, keep_theirs, w_here, w_there, feats,
    gr_ref, gc_ref, delta_ref, sums_ref, there_ref, here_ref, keep, acc, sums,
):
    step = pl.program_id(0)
    width = gm_ref.shape[1]
    half = width // 2
    unit, inv = norm(res_ref[...])
    upstream = gm_ref[...] + part_ref[...]
    back = norm_back(upstream, unit, inv, feats[1:2, :])
    gr_ref[...] = back
    put_halves(keep, me_ref[0], keep_mine[...].astype(f32), keep_theirs[...])
    g = (back * (keep[...] * (1 / 0.9))).astype(bf16)
    gc_ref[:, :half] = dot_nt(g, w_here[...]).astype(bf16)
    gc_ref[:, half:] = dot_nt(g, w_there[...]).astype(bf16)
    grad = dot_tn(ctx_ref[...], g)
    prod = gc_ref[...].astype(f32) * ctx_ref[...].astype(f32)
    high = prod.astype(bf16)
    rest = (prod - high.astype(f32)).astype(bf16)
    row = lax.broadcasted_iota(jnp.int32, (16, width), 0)
    lane = lax.broadcasted_iota(jnp.int32, (16, width), 1)
    pick = (lane // HEAD_DIM == (row & 7) * 2 + (row >> 3)).astype(bf16)
    delta_ref[...] = dot_nt(pick, high) + dot_nt(pick, rest)
    parts = [
        jnp.sum(g.astype(f32), axis=0, keepdims=True),
        jnp.sum(upstream * unit, axis=0, keepdims=True),
        jnp.sum(upstream, axis=0, keepdims=True),
        jnp.zeros((5, width), f32),
    ]
    row = jnp.concatenate(parts, axis=0)

    @pl.when(step == 0)
    def _():
        acc[...] = grad
        sums[...] = row

    @pl.when(step > 0)
    def _():
        acc[...] += grad
        sums[...] += row

    @pl.when(step == pl.num_programs(0) - 1)
    def _():
        here_ref[...] = acc[:half, :].astype(bf16)
        there_ref[...] = acc[half:, :].astype(bf16)
        sums_ref[...] = sums[...]


def out_back(me, gm, part, res, ctx, keep, w_here, w_there, feats, after):
    length, width = gm.shape
    half = width // 2
    steps = length // BLOCK
    band = lambda i, m: (i, 0)
    block = (BLOCK, width)
    return call(
        out_back_kernel, "out_back", (steps,), [me],
        [
            (gm, block, band),
            (part, block, band),
            (res, block, band),
            (ctx, block, band),
            (keep[0], (BLOCK, half), lambda i, m: (m[0] * steps + i, 0)),
            (keep[1], (BLOCK, half), band),
            (w_here, None, None),
            (w_there, None, None),
            (feats, None, None),
        ],
        [
            ((length, width), f32, block, band),
            ((length, width), bf16, block, band),
            ((16, length), f32, (16, BLOCK), lambda i, m: (0, i)),
            ((8, width), f32, None, None),
            ((half, width), bf16, None, None),
            ((half, width), bf16, None, None),
        ],
        [pltpu.VMEM((BLOCK, width), f32), pltpu.VMEM((width, width), f32), pltpu.VMEM((8, width), f32)],
        after=after,
    )


def qkv_last_kernel(
    me_ref, x_ref, dq, dk, dv, bias_here, bias_there, sums1, sums2, there_ref, here_ref, vh, vt, both,
):
    width = x_ref.shape[1]
    half = width // 2
    sums = []
    for c, g in enumerate((dq, dk, dv)):
        grad = dot_tn(x_ref[...], g[...]).astype(bf16)
        here_ref[c * width : (c + 1) * width, :] = grad[:, :half]
        there_ref[c * width : (c + 1) * width, :] = grad[:, half:]
        if c != 1:
            sums.append(jnp.sum(g[...].astype(f32), axis=0, keepdims=True))
    vh[...] = jnp.zeros_like(vh)
    vt[...] = jnp.zeros_like(vt)
    for side, (v, bias) in enumerate(((vh, bias_here), (vt, bias_there))):
        for row in range(2):
            v[row : row + 1, :] = sums[row][:, side * half : side * half + half]
        at = 2
        for n in range(bias.shape[1] // half):
            v[at : at + 1, :] = bias[:, n * half : (n + 1) * half]
            at += 1
    both[0:8, :] = sums1[...]
    both[8:16, :] = sums2[...]
    for v, m in ((vh, me_ref[0]), (vt, 1 - me_ref[0])):
        v[at : at + 3, :] = both[0:3, lanes_of(m, half)]
        v[at + 3 : at + 6, :] = both[8:11, lanes_of(m, half)]
    low = 3 * width
    for v, ref in ((vh, here_ref), (vt, there_ref)):
        ref[low : low + 16, :] = v[...].astype(bf16)
        ref[low + 16 :, :] = jnp.zeros((ref.shape[0] - low - 16, half), bf16)


def qkv_last(me, x, grads, bias_here, bias_there, sums1, sums2):
    width = x.shape[1]
    half = width // 2
    return call(
        qkv_last_kernel, "qkv_last", (1,), [me],
        [(a, None, None) for a in (x, *grads, bias_here, bias_there, sums1, sums2)],
        [((3 * width + 128, half), bf16, None, None)] * 2,
        [pltpu.VMEM((16, half), f32), pltpu.VMEM((16, half), f32), pltpu.VMEM((16, width), f32)],
    )


def tokens_back_kernel(me_ref, gr_ref, dq, dk, dv, w_here, w_there, mine_ref, theirs_ref, buf):
    half = mine_ref.shape[1]
    total = gr_ref[...]
    for c, g in enumerate((dq, dk, dv)):
        total = total + dot_nt(g[:, :half], w_here[c]) + dot_nt(g[:, half:], w_there[c])
    buf[...] = total
    mine_ref[...] = buf[:, lanes_of(me_ref[0], half)]
    theirs_ref[...] = buf[:, lanes_of(1 - me_ref[0], half)]


def tokens_back(me, gr, grads, w_here, w_there):
    length, width = gr.shape
    half = width // 2
    band = lambda i, m: (i, 0)
    return call(
        tokens_back_kernel, "tokens_back", (length // 512,), [me],
        [(a, (512, a.shape[1]), band) for a in (gr, *grads)] + [(w_here, None, None), (w_there, None, None)],
        [((length, half), f32, (512, half), band)] * 2,
        [pltpu.VMEM((512, width), f32)],
    )


def other(x):
    return lax.ppermute(x, "tensor", SWAP)


def across(x, mask, size):
    return lax.ppermute(x, "dp", [(i, i ^ mask) for i in range(size)])


def quarters_out(at, buf, outs, low=0):
    rows = outs[0].shape[0]
    for m, out in enumerate(outs):
        start = pl.multiple_of(low + (at ^ m) * rows, 8)
        out[...] = buf[pl.ds(start, rows), :].astype(bf16)


def last_quarters_kernel(cut_at, spot_ref, depth_ref, gq_here, gq_got, go_here, go_got, *refs):
    *outs, buf = refs
    rows, cols = gq_here.shape
    buf[:rows, :] = gq_here[...].astype(f32) + gq_got[...].astype(f32)
    half = go_here.shape[0]
    for side in range(2):
        lanes = slice(side * cols, side * cols + cols)
        low = rows + side * half
        buf[low : low + half, :] = go_here[:, lanes].astype(f32) + go_got[:, lanes].astype(f32)
    quarters_out(spot_ref[0], buf, outs[:4])
    quarters_out(depth_ref[0], buf, outs[4:], cut_at)


def last_quarters(spot, depth, gq_here, gq_got, go_here, go_got, cut_at):
    rows, cols = gq_here.shape
    rows += 2 * go_here.shape[0]
    arrays = (gq_here, gq_got, go_here, go_got)
    outs = call(
        functools.partial(last_quarters_kernel, cut_at), "last_quarters", (1,), [spot, depth],
        [(x, None, None) for x in arrays],
        [((n // 4, cols), bf16, None, None) for n in (cut_at, rows - cut_at) for _ in range(4)],
        [pltpu.VMEM((rows, cols), f32)],
    )
    return outs[:4], outs[4:]


def stage_kernel(jobs, here_ref, *refs):
    here = here_ref[0]
    places = {"spot": here & 3, "depth": here >> 2}
    n_ins = sum(n for _, n, _ in jobs)
    n_outs = sum(4 if kind.startswith("fold") else 1 for kind, _, _ in jobs)
    ins, outs, bufs = list(refs[:n_ins]), list(refs[n_ins : n_ins + n_outs]), list(refs[n_ins + n_outs :])
    for kind, n, axis in jobs:
        parts, ins = ins[:n], ins[n:]
        if kind == "total":
            outs.pop(0)[...] = sum_of(parts).astype(bf16)
            continue
        buf = bufs.pop(0)
        if kind == "fold":
            buf[...] = sum_of(parts)
            quarters_out(places[axis], buf, outs[:4])
            outs = outs[4:]
        else:
            rows = parts[0].shape[0]
            for m, part in enumerate(parts):
                start = pl.multiple_of((places[axis] ^ m) * rows, 8)
                buf[pl.ds(start, rows), :] = part[...].astype(f32)
            outs.pop(0)[...] = buf[...].astype(bf16)


def sum_of(refs):
    total = refs[0][...].astype(f32)
    for a in refs[1:]:
        total = total + a[...].astype(f32)
    return total


def stage(here, *jobs, after=()):
    outs, scratch, sizes = [], [], []
    for kind, parts, axis in jobs:
        rows, cols = parts[0].shape
        if kind == "fold":
            outs += [((rows // 4, cols), bf16, None, None)] * 4
            scratch.append(pltpu.VMEM((rows, cols), f32))
            sizes.append(4)
        elif kind == "total":
            outs.append(((rows, cols), bf16, None, None))
            sizes.append(1)
        else:
            outs.append(((len(parts) * rows, cols), bf16, None, None))
            scratch.append(pltpu.VMEM((len(parts) * rows, cols), f32))
            sizes.append(1)
    results = call(
        functools.partial(stage_kernel, [(kind, len(parts), axis) for kind, parts, axis in jobs]), "stage", (1,), [here],
        [(p, None, None) for _, parts, _ in jobs for p in parts], outs, scratch, after=after,
    )
    split = []
    for n in sizes:
        split.append(results[:n] if n > 1 else results[0])
        results = results[n:]
    return split if len(split) > 1 else split[0]


STEP = {"spot": 1, "depth": 4}


def swap(parts, axis, size):
    return [parts[0]] + [across(parts[m], m * STEP[axis], size) for m in (1, 2, 3)]


def share(x, axis, size):
    return swap([x] * 4, axis, size)


def plain_sum(at, quarters):
    whole = jnp.stack([lax.dynamic_index_in_dim(jnp.stack(quarters), at ^ m, 0, False) for m in range(4)])
    whole = lax.psum(whole, "dp")
    return [lax.dynamic_index_in_dim(whole, at ^ m, 0, False) for m in range(4)]


def place(buf, at, parts, low):
    rows = parts[0].shape[0]
    for m, q in enumerate(parts):
        buf[pl.ds(pl.multiple_of(low + (at ^ m) * rows, 8), rows), :] = q[...].astype(f32)


def end_kernel(at_ref, q0, q1, q2, q3, out):
    for m, q in enumerate((q0, q1, q2, q3)):
        @pl.when(pl.program_id(0) == m)
        def _():
            out[...] = q[...].astype(f32)


def end(at, quarters, name):
    rows, cols = quarters[0].shape
    return call(
        end_kernel, name, (4,), [at], [(q, None, None) for q in quarters],
        [((4 * rows, cols), f32, (rows, cols), lambda i, s: (s[0] ^ i, 0))],
    )[0]


def last_end_kernel(spot_ref, depth_ref, *refs):
    *quarters, qkv_ref, vec_ref, out_ref, buf = refs
    place(buf, spot_ref[0], quarters[:4], 0)
    place(buf, depth_ref[0], quarters[4:], 4 * quarters[0].shape[0])
    rows, cols = qkv_ref.shape[1:]
    for c in range(3):
        qkv_ref[c] = buf[c * rows : (c + 1) * rows, :]
    vec_ref[...] = buf[3 * rows : 3 * rows + 16, :]
    half = out_ref.shape[0]
    low = buf.shape[0] - 2 * half
    for side in range(2):
        out_ref[:, side * cols : side * cols + cols] = buf[low + side * half : low + (side + 1) * half, :]


def last_end(spot, depth, upper, lower, half):
    rows = 4 * (upper[0].shape[0] + lower[0].shape[0])
    cols = upper[0].shape[1]
    return call(
        last_end_kernel, "last_end", (1,), [spot, depth], [(q, None, None) for q in (*upper, *lower)],
        [((3, 2 * cols, cols), f32, None, None), ((16, cols), f32, None, None), ((half, 2 * cols), f32, None, None)],
        [pltpu.VMEM((rows, cols), f32)],
    )


def contrast(pooled_all, pool_w, pool_bias, log_temp, pairs_all):
    squash_float = jnp.tanh(dot_nn(pooled_all, pool_w) + pool_bias)
    squash = squash_float.astype(bf16).astype(f32)
    inv_norm = lax.rsqrt(jnp.sum(squash * squash, axis=-1, keepdims=True) + 1e-06)
    unit_all = squash * inv_norm
    temp = jnp.exp(-log_temp[0])
    logits = jnp.dot(unit_all, unit_all.T, precision=highest) * temp
    ids = jnp.arange(pooled_all.shape[0], dtype=jnp.int32)
    masked = jnp.where(ids[None, :] == ids[:, None], -1e30, logits)
    row_top = jnp.max(masked, axis=-1, keepdims=True)
    row_expo = jnp.exp(masked - row_top)
    row_total = jnp.sum(row_expo, axis=-1, keepdims=True)
    chosen = (ids[None, :] == pairs_all[:, None]).astype(f32)
    row_lse = row_top[:, 0] + jnp.log(row_total[:, 0])
    loss_total = jnp.sum(row_lse - jnp.sum(chosen * logits, axis=-1))
    grad_logits = row_expo / row_total - chosen
    grad_temp = -jnp.sum(grad_logits * logits)
    grad_unit = jnp.dot(grad_logits + grad_logits.T, unit_all, precision=highest) * temp
    grad_squash = inv_norm * (
        grad_unit - unit_all * jnp.sum(unit_all * grad_unit, axis=-1, keepdims=True)
    )
    grad_pool_pre = (grad_squash * (1.0 - squash_float * squash_float)).astype(bf16)
    return loss_total, grad_temp, grad_pool_pre


def contrast_kernel(
    count, rank_ref, me_ref, a_here, b_here, a_there, b_there, w_here, w_there, bias_ref, temp_ref, gw_ref, gb_ref,
    gp_ref, scalars_ref, all_ref, w_ref, pooled_ref, grad_ref,
):
    batch, width = pooled_ref.shape
    half = w_here.shape[0]
    me = me_ref[0]
    w_ref[pl.ds(pl.multiple_of(me * half, 128), half), :] = w_here[...]
    w_ref[pl.ds(pl.multiple_of((1 - me) * half, 128), half), :] = w_there[...]
    block = a_here.shape[0]
    rows_all = all_ref.shape[0]
    far = rank_ref[0] // (block // 8)
    for side, (a, b) in enumerate(((a_here, b_here), (a_there, b_there))):
        low = (me ^ side) * 2 * block
        all_ref[pl.ds(pl.multiple_of(low + far * block, 16), block), :] = a[...]
        all_ref[pl.ds(pl.multiple_of(low + (1 - far) * block, 16), block), :] = b[...]
    at = lax.broadcasted_iota(jnp.int32, (batch, rows_all), 1)
    row = lax.broadcasted_iota(jnp.int32, (batch, rows_all), 0)
    base = (row // count % 2) * 2 * block + (row // count // 2) * 16
    pooled = dot_nn((at == base + row % count).astype(bf16), all_ref[...]).astype(bf16)
    pooled_ref[...] = pooled
    upper = dot_nn((at == base + count).astype(bf16), all_ref[:, :128])
    lower = dot_nn((at == base + count + 1).astype(bf16), all_ref[:, :128])
    lane = lax.broadcasted_iota(jnp.int32, (batch, 128), 1)
    line = lax.broadcasted_iota(jnp.int32, (batch, 128), 0)
    partner = jnp.sum(jnp.where(lane == line % count, upper * 64.0 + lower, 0.0), axis=1, keepdims=True)
    squash_float = jnp.tanh(dot_nn(pooled, w_ref[...]) + bias_ref[...])
    squash = squash_float.astype(bf16).astype(f32)
    inv_norm = lax.rsqrt(jnp.sum(squash * squash, axis=-1, keepdims=True) + 1e-06)
    unit = squash * inv_norm
    temp = jnp.exp(-temp_ref[0:1, 0:1])
    logits = dot_nt(unit, unit, precision=highest) * temp
    ids = lax.broadcasted_iota(jnp.int32, (batch, batch), 1)
    masked = jnp.where(ids == lax.broadcasted_iota(jnp.int32, (batch, batch), 0), -1e30, logits)
    row_top = jnp.max(masked, axis=-1, keepdims=True)
    row_expo = jnp.exp(masked - row_top)
    row_total = jnp.sum(row_expo, axis=-1, keepdims=True)
    chosen = (ids.astype(f32) == partner).astype(f32)
    row_loss = row_top + jnp.log(row_total) - jnp.sum(chosen * logits, axis=-1, keepdims=True)
    loss = jnp.sum(row_loss, axis=0, keepdims=True) / batch
    grad_logits = row_expo / row_total - chosen
    grad_temp = -jnp.sum(jnp.sum(grad_logits * logits, axis=-1, keepdims=True), axis=0, keepdims=True)
    grad_unit = jnp.dot(
        grad_logits + grad_logits.T, unit, precision=highest, preferred_element_type=f32
    ) * temp
    grad_squash = inv_norm * (grad_unit - unit * jnp.sum(unit * grad_unit, axis=-1, keepdims=True))
    grad_pre = (grad_squash * (1.0 - squash_float * squash_float)).astype(bf16)
    gw_ref[...] = dot_tn(pooled_ref[:, lanes_of(me, half)], grad_pre)
    gb_ref[...] = jnp.sum(grad_pre.astype(f32), axis=0, keepdims=True)
    grad_ref[...] = grad_pre.astype(f32)
    own = grad_ref[pl.ds(pl.multiple_of(rank_ref[0] * count, 8), count), :].astype(bf16)
    gp_ref[...] = dot_nt(own, w_ref[...])
    spot = lax.broadcasted_iota(jnp.int32, (8, 128), 1)
    scalars_ref[...] = jnp.where(spot == 0, loss, grad_temp)


def contrast_call(rank, me, gathered, w_here, w_there, bias, log_temp, count):
    width = w_here.shape[1]
    rows_all = 4 * gathered[0].shape[0]
    batch = rows_all // 16 * count
    half = w_here.shape[0]
    temp = jnp.broadcast_to(log_temp.reshape(1, 1), (8, 128))
    return call(
        functools.partial(contrast_kernel, count), "contrast", (1,), [rank, me],
        [(a, None, None) for a in (*gathered, w_here, w_there, bias.reshape(1, width), temp)],
        [
            ((half, width), f32, None, None),
            ((1, width), f32, None, None),
            ((count, width), f32, None, None),
            ((8, 128), f32, None, None),
        ],
        [
            pltpu.VMEM((rows_all, width), bf16),
            pltpu.VMEM((width, width), bf16),
            pltpu.VMEM((batch, width), bf16),
            pltpu.VMEM((batch, width), f32),
        ],
    )


def per_device(
    dp_size,
    tokens,
    qkv_weight,
    qv_bias,
    out_weight,
    out_bias,
    first_gain,
    first_shift,
    up_weight,
    up_bias,
    down_weight,
    down_bias,
    second_gain,
    second_shift,
    pool_weight,
    pool_bias,
    log_temp,
    segments,
    cls_pos,
    pair_index,
    attn_keep,
    ffn_keep,
    grad_out,
):
    me = lax.axis_index("tensor")
    here = lax.axis_index("dp")
    length = segments.shape[1]
    half = tokens.shape[1]
    units = up_bias.shape[0]
    me_one = me.reshape(1).astype(jnp.int32)
    ORDER.clear()
    here_one = here.reshape(1).astype(jnp.int32)
    spot = here_one & 3

    def ordered(mine, theirs, axis):
        return jnp.where(
            me == 0,
            jnp.concatenate([mine, theirs], axis),
            jnp.concatenate([theirs, mine], axis),
        )

    x_there = other(their_rows(me_one, [tokens], length)[0])
    qkv_there = other(qkv_weight)
    vec = jnp.concatenate(
        [qv_bias.reshape(-1), up_bias, out_bias, first_gain, first_shift, down_bias, second_gain, second_shift]
    ).reshape(1, -1)
    out_there = other(out_weight)
    up_there = other(up_weight)
    down_there = other(down_weight)
    pool_there = other(pool_weight)

    seg = lax.dynamic_slice_in_dim(segments, me, 1, 0)
    col = jnp.broadcast_to(seg.reshape(length, 1), (length, 128))
    cls = lax.dynamic_slice_in_dim(cls_pos, me, 1, 0).reshape(-1)
    qv_full, up_b, feats = vectors(me_one, vec, other(vec), units, half)

    x, q, k, v = project(me_one, tokens, x_there, qkv_weight, qkv_there, qv_full, length)
    sends = their_rows(me_one, [attn_keep, ffn_keep, grad_out], length, [x])
    keep1 = (attn_keep, other(sends[0]))
    keep2 = (ffn_keep, other(sends[1]))
    go_there = other(sends[2])
    pooled = pooled_rows(
        me_one, seg, cls, pair_index, q, k, v, x, keep1, keep2,
        (out_weight, out_there, up_weight, up_there, down_weight, down_there), up_b, feats,
    )
    quick = dp_size == 16
    depth = here_one >> 2 if quick else here_one & 3
    if quick:
        near = stage(here_one, ("join", share(pooled, "spot", dp_size), "spot"))
        near_got = across(near, 4, dp_size)
    ctx, lse = attend(seg, col, q, k, v, [])
    if quick:
        part_a = jnp.where(
            here & 4 == 0, jnp.concatenate([near, near_got], 0), jnp.concatenate([near_got, near], 0)
        )
        part_b = across(part_a, 8, dp_size)
        part_a_there = other(part_a)
    res, low, act, slope, mixed, lay_mine, lay_theirs = feed_forward(
        me_one, ctx, x, out_weight, out_there, keep1, up_weight, up_there, down_weight, down_there, up_b, feats, keep2
    )
    layer_out = ordered(lay_mine, other(lay_theirs), 0)

    pool_rows = cls.shape[0]
    rank = here * 2 + me
    batch = dp_size * 2 * pool_rows
    if quick:
        grad_pool_w, grad_pool_b, grad_pooled, scalars = contrast_call(
            rank.reshape(1), me_one, [part_a, part_b, part_a_there, other(part_b)], pool_weight, pool_there,
            pool_bias, log_temp, pool_rows,
        )
        grad_pool_b = grad_pool_b.reshape(-1)
        loss, grad_temp = scalars[0, 0], scalars[0, 1]
    else:
        gathered = lax.all_gather(pooled, ("dp", "tensor"), axis=0, tiled=True)
        pool_w = ordered(pool_weight, pool_there, 0)
        gathered = gathered.reshape(-1, pooled.shape[0], D)
        pooled_all = gathered[:, :pool_rows].reshape(-1, D)
        numbers = gathered[:, pool_rows : pool_rows + 2, :pool_rows].astype(jnp.int32)
        pairs_all = (numbers[:, 0] * 64 + numbers[:, 1]).reshape(-1)
        loss_total, grad_temp, grad_pool_pre = contrast(pooled_all, pool_w, pool_bias, log_temp, pairs_all)
        loss = loss_total / batch
        pooled_half = lax.dynamic_slice_in_dim(pooled_all, me * half, half, 1)
        grad_pool_w = dot_tn(pooled_half, grad_pool_pre)
        grad_pool_b = jnp.sum(grad_pool_pre, axis=0, dtype=f32)
        grad_pooled = dot_nt(lax.dynamic_slice_in_dim(grad_pool_pre, rank * pool_rows, pool_rows, 0), pool_w)

    g, gm, sums2, gd_there = down_back(
        me_one, cls, mixed, grad_out, go_there, grad_pooled, feats, keep2, act
    )
    part, bias_there, gu_there = up_back(spot, low, g, slope, up_there, down_there, False)
    down = down_own(spot, act, g, other(gd_there))
    if quick:
        down = swap(down, "spot", dp_size)
    part, bias_here, *up = up_back(spot, low, g, slope, up_weight, down_weight, True, part, other(gu_there))
    gr, grad_ctx, delta, sums1, go_there, go_here = out_back(
        me_one, gm, part, res, ctx, keep1, out_weight, out_there, feats, down[1:3]
    )
    if quick:
        down = swap(stage(here_one, ("fold", down, "depth")), "depth", dp_size)
        up = swap(up, "spot", dp_size)
    go_got = other(go_there)
    grads = attend_back(seg, col, q, k, v, grad_ctx, lse, delta, tuple(range(D // PAIR)), [])
    if quick:
        down, up = stage(here_one, ("total", down, ""), ("fold", up, "depth"))
        down = share(down, "depth", dp_size)
        up = swap(up, "depth", dp_size)
    gq_there, gq_here = qkv_last(me_one, x, grads, bias_here, bias_there, sums1, sums2)
    gq_got = other(gq_there)
    gt_mine, gt_theirs = tokens_back(me_one, gr, grads, qkv_weight, qkv_there)
    upper, lower = last_quarters(spot, depth, gq_here, gq_got, go_here, go_got, 17 * 128)
    if quick:
        upper = swap(upper, "spot", dp_size)
        lower = swap(lower, "depth", dp_size)
        down, up = stage(here_one, ("join", down, "depth"), ("total", up, ""))
        down = share(down, "spot", dp_size)
        up = share(up, "depth", dp_size)
        upper, lower = stage(here_one, ("fold", upper, "depth"), ("fold", lower, "spot"))
        upper = swap(upper, "depth", dp_size)
        lower = swap(lower, "spot", dp_size)
        up = share(stage(here_one, ("join", up, "depth")), "spot", dp_size)
        upper, lower = stage(here_one, ("total", upper, ""), ("total", lower, ""))
        upper = share(upper, "depth", dp_size)
        lower = share(lower, "spot", dp_size)
    else:
        down, up, upper = [plain_sum(spot[0], a) for a in (down, up, upper)]
        lower = plain_sum(depth[0], lower)
    g_down_w = end(spot, down, "down_end")
    if quick:
        upper, lower = stage(here_one, ("join", upper, "depth"), ("join", lower, "spot"))
        upper = share(upper, "spot", dp_size)
        lower = share(lower, "depth", dp_size)
    g_up_w = end(spot, up, "up_end")
    g_qkv_w, vec_sum, g_out_w = last_end(spot, depth, upper, lower, half)
    grad_tokens = ordered(gt_mine, other(gt_theirs), 0)
    n_up = units // half
    return (
        layer_out,
        loss.reshape(1),
        grad_tokens,
        g_qkv_w,
        vec_sum[:2],
        g_out_w,
        vec_sum[2 + n_up],
        vec_sum[3 + n_up],
        vec_sum[4 + n_up],
        g_up_w,
        vec_sum[2 : 2 + n_up].reshape(-1),
        g_down_w,
        vec_sum[5 + n_up],
        vec_sum[6 + n_up],
        vec_sum[7 + n_up],
        grad_pool_w,
        grad_pool_b,
        grad_temp.reshape(1),
    )


def solution(mesh):
    return jax.shard_map(
        functools.partial(per_device, mesh.shape["dp"]),
        mesh=mesh,
        in_specs=(
            P("dp", "tensor"),
            P(None, None, "tensor"),
            P(None, "tensor"),
            P("tensor", None),
            P("tensor"),
            P("tensor"),
            P("tensor"),
            P(None, "tensor"),
            P("tensor"),
            P("tensor", None),
            P("tensor"),
            P("tensor"),
            P("tensor"),
            P("tensor", None),
            P(),
            P(),
            P("dp", None),
            P("dp", None),
            P("dp"),
            P("dp", "tensor"),
            P("dp", "tensor"),
            P("dp", "tensor"),
        ),
        out_specs=(
            P("dp", "tensor"),
            P(),
            P("dp", "tensor"),
            P(None, None, "tensor"),
            P(None, "tensor"),
            P("tensor", None),
            P("tensor"),
            P("tensor"),
            P("tensor"),
            P(None, "tensor"),
            P("tensor"),
            P("tensor", None),
            P("tensor"),
            P("tensor"),
            P("tensor"),
            P("tensor", None),
            P(),
            P(),
        ),
        check_vma=False,
    )
```

```python
import functools
import jax
import jax.numpy as jnp
from jax import lax
from jax.experimental import pallas as pl
from jax.experimental.pallas import tpu as pltpu
from jax.sharding import PartitionSpec as P

D = 768
HEAD_DIM = 64
PAIR = 2 * HEAD_DIM
BLOCK = 256
QROWS = 128
WIDE = QROWS + 512
NEAR = QROWS + 256
SWAP = [(0, 1), (1, 0)]
highest = lax.Precision.HIGHEST
f32 = jnp.float32
bf16 = jnp.bfloat16


def dot_nt(a, b, **kw):
    return lax.dot_general(a, b, (((1,), (1,)), ((), ())), preferred_element_type=f32, **kw)


def dot_tn(a, b):
    return lax.dot_general(a, b, (((0,), (0,)), ((), ())), preferred_element_type=f32)


def dot_nn(a, b):
    return jnp.dot(a, b, preferred_element_type=f32)


ORDER = []

MICROS = {
    "their_rows": 2, "both_rows": 2, "vectors": 1, "qkv": 5, "pooled": 9, "attend": 11, "ffn": 25, "contrast": 6, "down_back": 9,
    "down_own": 3.5, "up_back": 10, "up_own": 10, "out_back": 9, "attend_back": 21, "qkv_last": 4,
    "tokens_back": 5, "last_halves": 2, "stage": 1, "up_end": 3, "last_end": 3, "down_end": 3,
}


def norm(v):
    center = v - jnp.mean(v, axis=-1, keepdims=True)
    inv = lax.rsqrt(jnp.mean(center * center, axis=-1, keepdims=True) + 1e-06)
    return center * inv, inv


def norm_back(upstream, unit, inv, gain):
    scaled = upstream * gain
    return inv * (
        scaled
        - jnp.mean(scaled, axis=-1, keepdims=True)
        - unit * jnp.mean(scaled * unit, axis=-1, keepdims=True)
    )


def gelu_both(x):
    phi = 0.5 * (1.0 + lax.erf(x * (0.5 ** 0.5)))
    bell = jnp.exp(-0.5 * x * x) * 0.3989422804014327
    return x * phi, phi + x * bell


def lanes_of(me, half):
    return pl.ds(pl.multiple_of(me * half, 128), half)


def call(kernel, name, grid, scalars, ins, outs, scratch=(), vmem=26, after=(), aliases=None, free=False):
    after = [*after, *([] if free else ORDER[-1:])]
    n_scalars, n_ins, n_after = len(scalars), len(ins), len(after)

    def body(*refs):
        cut = n_scalars + n_ins
        kernel(*refs[:cut], *refs[cut + n_after :])

    def spec(shape, block, index):
        if block is None:
            zeros = (0,) * len(shape)
            return pl.BlockSpec(shape, lambda *a: zeros)
        return pl.BlockSpec(block, index)

    arrays = [a if b is None else pltpu.with_memory_space_constraint(a, pltpu.HBM) for a, b, _ in ins]
    result = pl.pallas_call(
        body,
        grid_spec=pltpu.PrefetchScalarGridSpec(
            num_scalar_prefetch=len(scalars),
            grid=grid,
            in_specs=[spec(a.shape, b, i) for a, b, i in ins]
            + [pl.BlockSpec(memory_space=pl.ANY)] * n_after,
            out_specs=[spec(s, b, i) for s, _, b, i in outs],
            scratch_shapes=list(scratch),
        ),
        out_shape=[jax.ShapeDtypeStruct(s, d) for s, d, _, _ in outs],
        compiler_params=pltpu.CompilerParams(vmem_limit_bytes=vmem << 20),
        cost_estimate=pl.CostEstimate(flops=int(MICROS[name] * 1.15e9), bytes_accessed=1000, transcendentals=0),
        input_output_aliases={n_scalars + i: o for i, o in (aliases or {}).items()},
        name=name,
    )(*scalars, *arrays, *after)
    if not free:
        ORDER.append(min(result, key=lambda r: r.size))
    return result


def put_halves(buf, me, mine, theirs):
    half = mine.shape[1]
    buf[:, lanes_of(me, half)] = mine.astype(buf.dtype)
    buf[:, lanes_of(1 - me, half)] = theirs.astype(buf.dtype)


def rows_kernel(me_ref, *refs):
    for i, o in zip(refs[: len(refs) // 2], refs[len(refs) // 2 :]):
        o[...] = i[...].astype(bf16)


def their_rows(me, arrays, length, after=()):
    half = arrays[0].shape[1]
    steps = length // 256
    return call(
        rows_kernel, "their_rows", (steps,), [me],
        [(a, (256, half), lambda i, m: ((1 - m[0]) * steps + i, 0)) for a in arrays],
        [((length, half), bf16, (256, half), lambda i, m: (i, 0))] * len(arrays),
        after=after,
    )


def both_rows_kernel(me_ref, mine, theirs, out):
    own = pl.program_id(0) // 2 == me_ref[0]

    @pl.when(own)
    def _():
        out[...] = mine[...]

    @pl.when(jnp.logical_not(own))
    def _():
        out[...] = theirs[...]


def both_rows(me, mine, theirs):
    length, half = mine.shape
    block = (length // 2, half)
    turn = lambda i, m: (i % 2, 0)
    return call(
        both_rows_kernel, "both_rows", (4,), [me], [(mine, block, turn), (theirs, block, turn)],
        [((2 * length, half), mine.dtype, block, lambda i, m: (i, 0))],
        free=True,
    )[0]


def vectors_kernel(units, me_ref, mine, theirs, qv_ref, up_ref, feats_ref):
    half = qv_ref.shape[1] // 2
    feats_ref[...] = jnp.zeros_like(feats_ref)
    for side, vec in enumerate((mine, theirs)):
        for row in range(2):
            qv_ref[row : row + 1, side * half : side * half + half] = vec[:, row * half : row * half + half]
        up_ref[:, side * units : side * units + units] = vec[:, 2 * half : 2 * half + units]
        spot = lanes_of(me_ref[0] if side == 0 else 1 - me_ref[0], half)
        for row in range(6):
            low = 2 * half + units + row * half
            feats_ref[row : row + 1, spot] = vec[:, low : low + half]


def vectors(me, mine, theirs, units, half):
    return call(
        functools.partial(vectors_kernel, units), "vectors", (1,), [me],
        [(mine, None, None), (theirs, None, None)],
        [((2, 2 * half), f32, None, None), ((1, 2 * units), f32, None, None), ((8, 2 * half), f32, None, None)],
    )


def qkv_kernel(me_ref, mine, theirs, w_here, w_there, bias, x_ref, q_ref, k_ref, v_ref):
    put_halves(x_ref, me_ref[0], mine[...], theirs[...])
    half = mine.shape[1]
    for c, out in enumerate((q_ref, k_ref, v_ref)):
        for side, w in enumerate((w_here, w_there)):
            cols = slice(side * half, side * half + half)
            y = dot_nn(x_ref[...], w[c])
            if c != 1:
                y = y + bias[c // 2 : c // 2 + 1, cols]
            out[:, cols] = y.astype(bf16)


def project(me, tokens, x_there, w_here, w_there, bias, length):
    half = tokens.shape[1]
    rows = 512
    steps = length // rows
    band = (rows, 2 * half)
    return call(
        qkv_kernel, "qkv", (steps,), [me],
        [
            (tokens, (rows, half), lambda i, m: (m[0] * steps + i, 0)),
            (x_there, (rows, half), lambda i, m: (i, 0)),
            (w_here, None, None),
            (w_there, None, None),
            (bias, None, None),
        ],
        [((length, 2 * half), bf16, band, lambda i, m: (i, 0))] * 4,
    )


def window_paths(step, length, seg_ref, run):
    first = step * QROWS
    near = pl.multiple_of(jnp.clip(first - 128, 0, length - NEAR), 128)
    left = seg_ref[jnp.maximum(near - 1, 0)] == seg_ref[first]
    right = seg_ref[jnp.minimum(near + NEAR, length - 1)] == seg_ref[first + QROWS - 1]
    spills = jnp.logical_or(
        jnp.logical_and(near > 0, left), jnp.logical_and(near + NEAR < length, right)
    )
    far = pl.multiple_of(jnp.clip(first - 256, 0, length - WIDE), 128)

    @pl.when(jnp.logical_not(spills))
    def _():
        run(NEAR, near)

    @pl.when(spills)
    def _():
        run(WIDE, far)


def fill_bias(bias_ref, col_ref, row_ref, width, start):
    bias = jnp.where(col_ref[pl.ds(start, width), :] == row_ref[...], 0.0, -1e30)
    for n in range(bias_ref.shape[1] // QROWS):
        bias_ref[0:width, n * QROWS : (n + 1) * QROWS] = bias


def head_mask(h):
    lane = lax.broadcasted_iota(jnp.int32, (1, PAIR), 1)
    return (lane // HEAD_DIM == h).astype(bf16)


def attend_kernel(length, pairs, seg_ref, col_ref, row_ref, q_ref, k_ref, v_ref, ctx_ref, lse_ref, bias_ref):
    def run(width, start):
        fill_bias(bias_ref, col_ref, row_ref, width, start)
        rows = pl.ds(start, width)
        for j in range(pairs):
            lanes = slice(j * PAIR, j * PAIR + PAIR)
            q2 = q_ref[:, lanes] * bf16(HEAD_DIM ** (-0.5))
            keys = k_ref[rows, lanes]
            values = v_ref[rows, lanes]
            parts = []
            for h in range(2):
                scores = dot_nt(keys, q2 * head_mask(h)) + bias_ref[0:width, :]
                top = jnp.max(scores, axis=0, keepdims=True)
                expo = jnp.exp(scores - top)
                total = jnp.sum(expo, axis=0, keepdims=True)
                out = dot_tn(values, expo.astype(bf16))[h * HEAD_DIM : (h + 1) * HEAD_DIM]
                parts.append(out * (1.0 / total))
                lse_ref[8 * h + j : 8 * h + j + 1, :] = top + jnp.log(total)
            ctx_ref[:, lanes] = jnp.concatenate(parts, axis=0).T.astype(bf16)

    window_paths(pl.program_id(0), length, seg_ref, run)


def attend(seg, col, q, k, v, after):
    length, width = q.shape
    band = lambda i, s: (i, 0)
    block = (QROWS, width)
    return call(
        functools.partial(attend_kernel, length, width // PAIR), "attend", (length // QROWS,),
        [seg.reshape(length)],
        [
            (col, None, None),
            (seg.reshape(1, length), (1, QROWS), lambda i, s: (0, i)),
            (q, block, band),
            (k, None, None),
            (v, None, None),
        ],
        [
            ((length, width), bf16, block, band),
            ((16, length), f32, (16, QROWS), lambda i, s: (0, i)),
        ],
        [pltpu.VMEM((WIDE, QROWS), f32)],
        after=after,
    )


def attend_back_kernel(
    length, chosen, seg_ref, col_ref, row_ref, q_ref, k_ref, v_ref, do_ref, lse_ref, delta_ref,
    dq_ref, dk_ref, dv_ref, bias_ref, dk_acc, dv_acc,
):
    step = pl.program_id(0)

    @pl.when(step == 0)
    def _():
        dk_acc[...] = jnp.zeros_like(dk_acc)
        dv_acc[...] = jnp.zeros_like(dv_acc)

    def both(ref, j):
        return jnp.concatenate([ref[j : j + 1, :], ref[8 + j : 9 + j, :]], axis=1)

    def run(width, start):
        fill_bias(bias_ref, col_ref, row_ref, width, start)
        rows = pl.ds(start, width)
        for n, j in enumerate(chosen):
            lanes = slice(j * PAIR, j * PAIR + PAIR)
            slot = slice(n * PAIR, n * PAIR + PAIR)
            q2 = q_ref[:, lanes] * bf16(HEAD_DIM ** (-0.5))
            do2 = do_ref[:, lanes]
            keys = k_ref[rows, lanes]
            values = v_ref[rows, lanes]
            queries = jnp.concatenate([q2 * head_mask(0), q2 * head_mask(1)], axis=0)
            grads = jnp.concatenate([do2 * head_mask(0), do2 * head_mask(1)], axis=0)
            scores = dot_nt(keys, queries) + bias_ref[0:width, :]
            probs = jnp.exp(scores - both(lse_ref, j))
            grad_probs = dot_nt(values, grads)
            grad_scores = (probs * (grad_probs - both(delta_ref, j))).astype(bf16)
            dv_acc[rows, slot] += dot_nn(probs.astype(bf16), grads)
            dk_acc[rows, slot] += dot_nn(grad_scores, queries)
            dq = dot_tn(keys, grad_scores)
            dq = jnp.concatenate([dq[:HEAD_DIM, :QROWS], dq[HEAD_DIM:, QROWS:]], axis=0).T
            dq_ref[:, slot] = (dq * (HEAD_DIM ** (-0.5))).astype(bf16)

    window_paths(step, length, seg_ref, run)

    @pl.when(step == length // QROWS - 1)
    def _():
        dk_ref[...] = dk_acc[...].astype(bf16)
        dv_ref[...] = dv_acc[...].astype(bf16)


def attend_back(seg, col, q, k, v, grad_ctx, lse, delta, chosen, after):
    length, width = q.shape
    cols = len(chosen) * PAIR
    block = (QROWS, width)
    band = lambda i, s: (i, 0)
    flat = lambda i, s: (0, i)
    whole = ((length, cols), bf16, None, None)
    return call(
        functools.partial(attend_back_kernel, length, chosen), "attend_back", (length // QROWS,),
        [seg.reshape(length)],
        [
            (col, None, None),
            (seg.reshape(1, length), (1, QROWS), flat),
            (q, block, band),
            (k, None, None),
            (v, None, None),
            (grad_ctx, block, band),
            (lse, (16, QROWS), flat),
            (delta, (16, QROWS), flat),
        ],
        [((length, cols), bf16, (QROWS, cols), band), whole, whole],
        [
            pltpu.VMEM((WIDE, 2 * QROWS), f32),
            pltpu.VMEM((length, cols), f32),
            pltpu.VMEM((length, cols), f32),
        ],
        after=after,
    )


UNITS = 512
FROWS = 512


def sides(sides_count, step, here_first, run_here, run_there):
    low, high = (run_here, run_there) if here_first else (run_there, run_here)

    @pl.when(step < sides_count)
    def _():
        low()

    @pl.when(step >= sides_count)
    def _():
        high()


def ffn_kernel(
    count, me_ref, cls_ref, pair_ref, ctx_ref, x_ref, ow_here, ow_there, keep1_mine, keep1_theirs, uw_here, uw_there, dw_here,
    dw_there, up_b, feats, keep_mine, keep_theirs, res_ref, low_ref, act_ref, slope_ref, mixed_ref, mine_ref,
    theirs_ref, pooled_ref, keep, value_buf,
):
    step = pl.program_id(0)
    length = low_ref.shape[0]

    @pl.when(step == 0)
    def _():
        mixed_ref[...] = jnp.zeros_like(mixed_ref)
        side = ow_here.shape[0]
        for r in range(length // BLOCK):
            rows = slice(r * BLOCK, (r + 1) * BLOCK)
            put_halves(keep, me_ref[0], keep1_mine[rows, :].astype(f32), keep1_theirs[rows, :])
            branch = dot_nn(ctx_ref[rows, :side], ow_here[...]) + dot_nn(ctx_ref[rows, side:], ow_there[...])
            residual = x_ref[rows, :].astype(f32) + (branch + feats[0:1, :]) * (keep[...] * (1 / 0.9))
            res_ref[rows, :] = residual
            low_ref[rows, :] = (norm(residual)[0] * feats[1:2, :] + feats[2:3, :]).astype(bf16)

    def run(up, down):
        def go():
            for r in range(length // FROWS):
                rows = slice(r * FROWS, (r + 1) * FROWS)
                pre = dot_nn(low_ref[rows, :], up[...]) + up_b[...]
                value, slope = gelu_both(pre)
                value = value.astype(bf16)
                act_ref[rows, :] = value
                slope_ref[rows, :] = slope.astype(bf16)
                mixed_ref[rows, :] += dot_nn(value, down[...])

        return go

    sides(count, step, True, run(uw_here, dw_here), run(uw_there, dw_there))

    @pl.when(step == 2 * count - 1)
    def _():
        half = mine_ref.shape[1]
        me = me_ref[0]
        width = value_buf.shape[1]
        chosen = cls_ref.shape[0]
        line = lax.broadcasted_iota(jnp.int32, (16, BLOCK), 0)
        spot = jnp.full((16, BLOCK), -1, jnp.int32)
        for c in range(chosen):
            spot = jnp.where(line == c, cls_ref[c], spot)
        line = lax.broadcasted_iota(jnp.int32, (16, width), 0)
        lane = lax.broadcasted_iota(jnp.int32, (16, width), 1)
        numbers = jnp.zeros((16, width), jnp.int32)
        for c in range(chosen):
            number = pair_ref[me * chosen + c]
            numbers = jnp.where((lane == c) & (line == chosen), number // 64, numbers)
            numbers = jnp.where((lane == c) & (line == chosen + 1), number % 64, numbers)
        pooled = numbers.astype(f32)
        for r in range(length // BLOCK):
            rows = slice(r * BLOCK, (r + 1) * BLOCK)
            put_halves(keep, me, keep_mine[rows, :].astype(f32), keep_theirs[rows, :])
            hidden = norm(res_ref[rows, :])[0] * feats[1:2, :] + feats[2:3, :]
            mixed = hidden + (mixed_ref[rows, :] + feats[3:4, :]) * (keep[...] * (1 / 0.9))
            mixed_ref[rows, :] = mixed
            value_buf[...] = (norm(mixed)[0] * feats[4:5, :] + feats[5:6, :]).astype(bf16)
            here = lax.broadcasted_iota(jnp.int32, (16, BLOCK), 1) + r * BLOCK
            pooled = pooled + dot_nn((here == spot).astype(bf16), value_buf[...])
            mine_ref[rows, :] = value_buf[:, lanes_of(me, half)]
            theirs_ref[rows, :] = value_buf[:, lanes_of(1 - me, half)]
        pooled_ref[...] = pooled.astype(bf16)


def feed_forward(me, cls, pair_index, ctx, x, ow_here, ow_there, keep1, uw_here, uw_there, dw_here, dw_there, up_b, feats, keep):
    length, width = x.shape
    half = width // 2
    count = uw_here.shape[1] // UNITS
    units = 2 * uw_here.shape[1]
    first = lambda i: jnp.minimum(i, count - 1)
    second = lambda i: jnp.maximum(i - count, 0)
    return call(
        functools.partial(ffn_kernel, count), "ffn", (2 * count,), [me, cls, pair_index],
        [
            (ctx, None, None),
            (x, None, None),
            (ow_here, None, None),
            (ow_there, None, None),
            (keep1[0], (length, half), lambda i, m, c, p: (m[0], 0)),
            (keep1[1], None, None),
            (uw_here, (width, UNITS), lambda i, m, c, p: (0, first(i))),
            (uw_there, (width, UNITS), lambda i, m, c, p: (0, second(i))),
            (dw_here, (UNITS, width), lambda i, m, c, p: (first(i), 0)),
            (dw_there, (UNITS, width), lambda i, m, c, p: (second(i), 0)),
            (up_b, (1, UNITS), lambda i, m, c, p: (0, i)),
            (feats, None, None),
            (keep[0], (length, half), lambda i, m, c, p: (m[0], 0)),
            (keep[1], None, None),
        ],
        [
            ((length, width), f32, None, None),
            ((length, width), bf16, None, None),
            ((length, units), bf16, (length, UNITS), lambda i, m, c, p: (0, i)),
            ((length, units), bf16, (length, UNITS), lambda i, m, c, p: (0, i)),
            ((length, width), f32, None, None),
            ((length, half), bf16, None, None),
            ((length, half), bf16, None, None),
            ((16, width), bf16, None, None),
        ],
        [pltpu.VMEM((BLOCK, width), f32), pltpu.VMEM((BLOCK, width), bf16)],
        vmem=36,
    )


def down_back_kernel(
    me_ref, cls_ref, mixed_ref, go_mine, go_theirs, pooled_ref, feats, keep_mine, keep_theirs, act_ref,
    g_ref, gm_ref, sums_ref, there_ref, buf, keep,
):
    length, width = mixed_ref.shape

    @pl.when(pl.program_id(0) == 0)
    def _():
        me = me_ref[0]
        put_halves(buf, me, go_mine[...].astype(f32), go_theirs[...])
        for c in range(cls_ref.shape[0]):
            spot = pl.ds(cls_ref[c], 1)
            buf[spot, :] = buf[spot, :] + pooled_ref[c : c + 1, :]
        gain_sum = jnp.zeros((1, width), f32)
        shift_sum = jnp.zeros((1, width), f32)
        bias_sum = jnp.zeros((1, width), f32)
        for r in range(length // BLOCK):
            rows = slice(r * BLOCK, (r + 1) * BLOCK)
            upstream = buf[rows, :]
            unit, inv = norm(mixed_ref[rows, :])
            back = norm_back(upstream, unit, inv, feats[4:5, :])
            gm_ref[rows, :] = back
            put_halves(keep, me, keep_mine[rows, :].astype(f32), keep_theirs[rows, :])
            g = (back * (keep[...] * (1 / 0.9))).astype(bf16)
            g_ref[rows, :] = g
            gain_sum = gain_sum + jnp.sum(upstream * unit, axis=0, keepdims=True)
            shift_sum = shift_sum + jnp.sum(upstream, axis=0, keepdims=True)
            bias_sum = bias_sum + jnp.sum(g.astype(f32), axis=0, keepdims=True)
        sums_ref[...] = jnp.concatenate(
            [bias_sum, gain_sum, shift_sum, jnp.zeros((5, width), f32)], axis=0
        )

    there_ref[...] = dot_tn(act_ref[...], g_ref[...]).astype(bf16)


def down_back(me, cls, mixed, go_arg, go_there, grad_pooled, feats, keep, act):
    length, width = mixed.shape
    half = width // 2
    units = act.shape[1] // 2
    count = units // UNITS
    part = lambda a: (a, (length, half), lambda i, m, c: (m[0], 0))
    return call(
        down_back_kernel, "down_back", (count,), [me, cls],
        [
            (mixed, None, None),
            part(go_arg),
            (go_there, None, None),
            (grad_pooled, None, None),
            (feats, None, None),
            part(keep[0]),
            (keep[1], None, None),
            (act, (length, UNITS), lambda i, m, c: (0, i + count)),
        ],
        [
            ((length, width), bf16, None, None),
            ((length, width), f32, None, None),
            ((8, width), f32, None, None),
            ((units, width), bf16, (UNITS, width), lambda i, m, c: (i, 0)),
        ],
        [pltpu.VMEM((length, width), f32), pltpu.VMEM((BLOCK, width), f32)],
    )


def down_own_kernel(bit_ref, act_ref, g_ref, got_ref, keep_ref, send_ref):
    grad = (dot_tn(act_ref[...], g_ref[...]) + got_ref[...].astype(f32)).astype(bf16)
    mine = pl.program_id(0) == bit_ref[0]

    @pl.when(mine)
    def _():
        keep_ref[...] = grad

    @pl.when(jnp.logical_not(mine))
    def _():
        send_ref[...] = grad


def down_own(bit, act, g, got):
    length, width = g.shape
    rows = got.shape[0] // 2
    return call(
        down_own_kernel, "down_own", (2,), [bit],
        [
            (act, (length, rows), lambda i, s: (0, i)),
            (g, None, None),
            (got, (rows, width), lambda i, s: (i, 0)),
        ],
        [((rows, width), bf16, None, None)] * 2,
    )


def up_back_kernel(
    own, bit_ref, low_ref, g_ref, slope_ref, up, down, *refs,
):
    if own:
        start_ref, got_ref, part_ref, bias_ref, *out_refs, grad_buf = refs
    else:
        part_ref, bias_ref, out_ref = refs
    step = pl.program_id(0)
    length, width = g_ref.shape

    @pl.when(step == 0)
    def _():
        part_ref[...] = start_ref[...] if own else jnp.zeros_like(part_ref)

    total = jnp.zeros((1, UNITS), f32)
    grads = []
    for r in range(length // FROWS):
        rows = slice(r * FROWS, (r + 1) * FROWS)
        gu = (dot_nt(g_ref[rows, :], down[...]) * slope_ref[rows, :].astype(f32)).astype(bf16)
        total = total + jnp.sum(gu.astype(f32), axis=0, keepdims=True)
        part_ref[rows, :] += dot_nt(gu, up[...])
        grads.append(gu)
    bias_ref[...] = total
    grad = dot_tn(low_ref[...], jnp.concatenate(grads, axis=0))
    if own:
        grad_buf[...] = (grad + got_ref[...].astype(f32)).astype(bf16)
        halves_out(bit_ref[0], grad_buf, out_refs)
    else:
        out_ref[...] = grad.astype(bf16)


def up_back(bit, low, g, slope, up, down, own, start=None, got=None, after=()):
    length, width = g.shape
    units = up.shape[1]
    count = units // UNITS
    skip = 0 if own else count
    ins = [
        (low, None, None),
        (g, None, None),
        (slope, (length, UNITS), lambda i, s: (0, i + skip)),
        (up, (width, UNITS), lambda i, s: (0, i)),
        (down, (UNITS, width), lambda i, s: (i, 0)),
    ]
    rows = width // 2 if own else width
    outs = [
        ((length, width), f32, None, None),
        ((1, units), f32, (1, UNITS), lambda i, s: (0, i)),
    ] + [((rows, units), bf16, (rows, UNITS), lambda i, s: (0, i))] * (width // rows)
    scratch = []
    if own:
        scratch = [pltpu.VMEM((width, UNITS), bf16)]
        ins += [(start, None, None), (got, (width, UNITS), lambda i, s: (0, i))]
    return call(
        functools.partial(up_back_kernel, own), "up_own" if own else "up_back", (count,), [bit], ins, outs, scratch,
        after=after,
    )


def out_back_kernel(
    me_ref, gm_ref, part_ref, res_ref, ctx_ref, keep_mine, keep_theirs, w_here, w_there, feats,
    gr_ref, gc_ref, delta_ref, sums_ref, there_ref, here_ref, keep, acc, sums,
):
    step = pl.program_id(0)
    width = gm_ref.shape[1]
    half = width // 2
    rows = pl.ds(pl.multiple_of(step * BLOCK, BLOCK), BLOCK)
    unit, inv = norm(res_ref[rows, :])
    upstream = gm_ref[rows, :] + part_ref[rows, :]
    back = norm_back(upstream, unit, inv, feats[1:2, :])
    gr_ref[...] = back
    put_halves(keep, me_ref[0], keep_mine[...].astype(f32), keep_theirs[...])
    g = (back * (keep[...] * (1 / 0.9))).astype(bf16)
    gc_ref[:, :half] = dot_nt(g, w_here[...]).astype(bf16)
    gc_ref[:, half:] = dot_nt(g, w_there[...]).astype(bf16)
    grad = dot_tn(ctx_ref[...], g)
    prod = gc_ref[...].astype(f32) * ctx_ref[...].astype(f32)
    high = prod.astype(bf16)
    rest = (prod - high.astype(f32)).astype(bf16)
    row = lax.broadcasted_iota(jnp.int32, (16, width), 0)
    lane = lax.broadcasted_iota(jnp.int32, (16, width), 1)
    pick = (lane // HEAD_DIM == (row & 7) * 2 + (row >> 3)).astype(bf16)
    delta_ref[...] = dot_nt(pick, high) + dot_nt(pick, rest)
    parts = [
        jnp.sum(g.astype(f32), axis=0, keepdims=True),
        jnp.sum(upstream * unit, axis=0, keepdims=True),
        jnp.sum(upstream, axis=0, keepdims=True),
        jnp.zeros((5, width), f32),
    ]
    row = jnp.concatenate(parts, axis=0)

    @pl.when(step == 0)
    def _():
        acc[...] = grad
        sums[...] = row

    @pl.when(step > 0)
    def _():
        acc[...] += grad
        sums[...] += row

    @pl.when(step == pl.num_programs(0) - 1)
    def _():
        here_ref[...] = acc[:half, :].astype(bf16)
        there_ref[...] = acc[half:, :].astype(bf16)
        sums_ref[...] = sums[...]


def out_back(me, gm, part, res, ctx, keep, w_here, w_there, feats, after):
    length, width = gm.shape
    half = width // 2
    steps = length // BLOCK
    band = lambda i, m: (i, 0)
    block = (BLOCK, width)
    return call(
        out_back_kernel, "out_back", (steps,), [me],
        [
            (gm, None, None),
            (part, None, None),
            (res, None, None),
            (ctx, block, band),
            (keep[0], (BLOCK, half), lambda i, m: (m[0] * steps + i, 0)),
            (keep[1], (BLOCK, half), band),
            (w_here, None, None),
            (w_there, None, None),
            (feats, None, None),
        ],
        [
            ((length, width), f32, block, band),
            ((length, width), bf16, block, band),
            ((16, length), f32, (16, BLOCK), lambda i, m: (0, i)),
            ((8, width), f32, None, None),
            ((half, width), bf16, None, None),
            ((half, width), bf16, None, None),
        ],
        [pltpu.VMEM((BLOCK, width), f32), pltpu.VMEM((width, width), f32), pltpu.VMEM((8, width), f32)],
        after=after,
    )


def qkv_last_kernel(
    me_ref, x_ref, dq, dk, dv, bias_here, bias_there, sums1, sums2, there_ref, here_ref, vh, vt, both,
):
    width = x_ref.shape[1]
    half = width // 2
    sums = []
    for c, g in enumerate((dq, dk, dv)):
        grad = dot_tn(x_ref[...], g[...]).astype(bf16)
        here_ref[c * width : (c + 1) * width, :] = grad[:, :half]
        there_ref[c * width : (c + 1) * width, :] = grad[:, half:]
        if c != 1:
            sums.append(jnp.sum(g[...].astype(f32), axis=0, keepdims=True))
    vh[...] = jnp.zeros_like(vh)
    vt[...] = jnp.zeros_like(vt)
    for side, (v, bias) in enumerate(((vh, bias_here), (vt, bias_there))):
        for row in range(2):
            v[row : row + 1, :] = sums[row][:, side * half : side * half + half]
        at = 2
        for n in range(bias.shape[1] // half):
            v[at : at + 1, :] = bias[:, n * half : (n + 1) * half]
            at += 1
    both[0:8, :] = sums1[...]
    both[8:16, :] = sums2[...]
    for v, m in ((vh, me_ref[0]), (vt, 1 - me_ref[0])):
        v[at : at + 3, :] = both[0:3, lanes_of(m, half)]
        v[at + 3 : at + 6, :] = both[8:11, lanes_of(m, half)]
    low = 3 * width
    for v, ref in ((vh, here_ref), (vt, there_ref)):
        ref[low : low + 16, :] = v[...].astype(bf16)
        ref[low + 16 :, :] = jnp.zeros((ref.shape[0] - low - 16, half), bf16)


def qkv_last(me, x, grads, bias_here, bias_there, sums1, sums2):
    width = x.shape[1]
    half = width // 2
    return call(
        qkv_last_kernel, "qkv_last", (1,), [me],
        [(a, None, None) for a in (x, *grads, bias_here, bias_there, sums1, sums2)],
        [((3 * width + 128, half), bf16, None, None)] * 2,
        [pltpu.VMEM((16, half), f32), pltpu.VMEM((16, half), f32), pltpu.VMEM((16, width), f32)],
    )


def tokens_back_kernel(me_ref, gr_ref, dq, dk, dv, w_here, w_there, mine_ref, theirs_ref, buf):
    half = mine_ref.shape[1]
    total = gr_ref[...]
    rows = pl.ds(pl.multiple_of(pl.program_id(0) * 512, 512), 512)
    for c, g in enumerate((dq[...], dk[rows, :], dv[rows, :])):
        total = total + dot_nt(g[:, :half], w_here[c]) + dot_nt(g[:, half:], w_there[c])
    buf[...] = total
    mine_ref[...] = buf[:, lanes_of(me_ref[0], half)]
    theirs_ref[...] = buf[:, lanes_of(1 - me_ref[0], half)]


def tokens_back(me, gr, grads, w_here, w_there):
    length, width = gr.shape
    half = width // 2
    band = lambda i, m: (i, 0)
    return call(
        tokens_back_kernel, "tokens_back", (length // 512,), [me],
        [(a, (512, width), band) for a in (gr, grads[0])]
        + [(a, None, None) for a in (*grads[1:], w_here, w_there)],
        [((length, half), f32, (512, half), band)] * 2,
        [pltpu.VMEM((512, width), f32)],
    )


def other(x):
    return lax.ppermute(x, "tensor", SWAP)


def across(x, mask, size):
    return lax.ppermute(x, "dp", [(i, i ^ mask) for i in range(size)])


def halves_out(at, buf, outs, low=0):
    rows = outs[0].shape[0]
    for m, out in enumerate(outs):
        start = pl.multiple_of(low + (at ^ m) * rows, 8)
        out[...] = buf[pl.ds(start, rows), :].astype(bf16)


def last_halves_kernel(cuts, here_ref, gq_here, gq_got, go_here, go_got, *refs):
    *outs, buf = refs
    rows, cols = gq_here.shape
    buf[:rows, :] = gq_here[...].astype(f32) + gq_got[...].astype(f32)
    half = go_here.shape[0]
    for side in range(2):
        lanes = slice(side * cols, side * cols + cols)
        low = rows + side * half
        buf[low : low + half, :] = go_here[:, lanes].astype(f32) + go_got[:, lanes].astype(f32)
    low = 0
    for n, (high, bit) in enumerate(cuts):
        halves_out((here_ref[0] >> bit) & 1, buf, outs[2 * n : 2 * n + 2], low)
        low = high


def last_halves(here, gq_here, gq_got, go_here, go_got, cuts):
    rows, cols = gq_here.shape
    rows += 2 * go_here.shape[0]
    lows = [0] + [high for high, _ in cuts[:-1]]
    outs = call(
        functools.partial(last_halves_kernel, cuts), "last_halves", (1,), [here],
        [(x, None, None) for x in (gq_here, gq_got, go_here, go_got)],
        [(((high - low) // 2, cols), bf16, None, None) for low, (high, _) in zip(lows, cuts) for _ in range(2)],
        [pltpu.VMEM((rows, cols), f32)],
    )
    return [outs[2 * n : 2 * n + 2] for n in range(len(cuts))]


def sum_of(refs):
    total = refs[0][...].astype(f32)
    for a in refs[1:]:
        total = total + a[...].astype(f32)
    return total


def stage_kernel(jobs, here_ref, *refs):
    n_ins = sum(n for _, n, _, _ in jobs)
    n_outs = sum(2 if kind == "fold" else 1 for kind, _, _, _ in jobs)
    ins, outs, bufs = list(refs[:n_ins]), list(refs[n_ins : n_ins + n_outs]), list(refs[n_ins + n_outs :])
    for kind, n, bit, many in jobs:
        parts, ins = ins[:n], ins[n:]
        if kind == "total":
            outs.pop(0)[...] = sum_of(parts).astype(bf16)
            continue
        at = (here_ref[0] >> bit) & (many - 1)
        buf = bufs.pop(0)
        if kind == "fold":
            buf[...] = sum_of(parts)
            halves_out(at, buf, outs[:2])
            outs = outs[2:]
        else:
            place(buf, at, parts, 0)
            outs.pop(0)[...] = buf[...].astype(bf16)


def stage(here, *jobs, free=False):
    outs, scratch, counts = [], [], []
    for kind, parts, _ in jobs:
        rows, cols = parts[0].shape
        if kind == "fold":
            outs += [((rows // 2, cols), bf16, None, None)] * 2
            scratch.append(pltpu.VMEM((rows, cols), f32))
        elif kind == "total":
            outs.append(((rows, cols), bf16, None, None))
        else:
            outs.append(((len(parts) * rows, cols), bf16, None, None))
            scratch.append(pltpu.VMEM((len(parts) * rows, cols), f32))
        counts.append(2 if kind == "fold" else 1)
    results = call(
        functools.partial(stage_kernel, [(kind, len(parts), bit, len(parts)) for kind, parts, bit in jobs]), "stage",
        (1,), [here], [(p, None, None) for _, parts, _ in jobs for p in parts], outs, scratch, free=free,
    )
    split = []
    for n in counts:
        split.append(results[:n] if n > 1 else results[0])
        results = results[n:]
    return split


class Chain:
    def __init__(self, halves, order, size):
        self.order, self.size, self.step = order, size, 0
        self.parts = halves
        self.send(halves[1])

    def send(self, x):
        bit = self.order[self.step]
        self.parts = [self.parts[0], across(x, 1 << bit, self.size)]

    def job(self):
        last = len(self.order) - 1
        if self.step < last:
            return ("fold", self.parts, self.order[self.step + 1])
        if self.step == last:
            return ("total", self.parts, 0)
        return ("join", self.parts, self.order[2 * last + 1 - self.step])

    def take(self, result):
        last = len(self.order) - 1
        self.step += 1
        if self.step <= last:
            self.parts = result
            bit, x = self.order[self.step], result[1]
        else:
            self.parts = [result, result]
            bit, x = self.order[2 * last + 1 - self.step], result
        self.parts = [self.parts[0], across(x, 1 << bit, self.size)]


def advance(here, *chains, free=False):
    for chain, result in zip(chains, stage(here, *[c.job() for c in chains], free=free)):
        chain.take(result)


def plain_sum(at, halves):
    whole = jnp.where(at == 0, jnp.stack(halves), jnp.stack(halves[::-1]))
    whole = lax.psum(whole, "dp")
    return jnp.where(at == 0, whole, whole[::-1])


def place(buf, at, parts, low):
    rows = parts[0].shape[0]
    for m, q in enumerate(parts):
        buf[pl.ds(pl.multiple_of(low + (at ^ m) * rows, 8), rows), :] = q[...].astype(buf.dtype)


def end_kernel(at_ref, mine, theirs, out):
    mine_now = pl.program_id(0) // 2 == at_ref[0]
    rows = out.shape[0]
    low = pl.multiple_of(pl.program_id(0) % 2 * rows, 16)

    @pl.when(mine_now)
    def _():
        out[...] = mine[pl.ds(low, rows), :].astype(f32)

    @pl.when(jnp.logical_not(mine_now))
    def _():
        out[...] = theirs[pl.ds(low, rows), :].astype(f32)


def end(at, halves, name):
    rows, cols = halves[0].shape
    return call(
        end_kernel, name, (4,), [at], [(q, None, None) for q in halves],
        [((2 * rows, cols), f32, (rows // 2, cols), lambda i, s: (i, 0))],
        free=True,
    )[0]


def last_end_kernel(bits, here_ref, *refs):
    *halves, qkv_ref, vec_ref, out_ref, buf = refs
    low = 0
    for n, bit in enumerate(bits):
        place(buf, (here_ref[0] >> bit) & 1, halves[2 * n : 2 * n + 2], low)
        low += 2 * halves[2 * n].shape[0]
    rows, cols = qkv_ref.shape[1:]
    for c in range(3):
        qkv_ref[c] = buf[c * rows : (c + 1) * rows, :]
    vec_ref[...] = buf[3 * rows : 3 * rows + 16, :]
    half = out_ref.shape[0]
    low = buf.shape[0] - 2 * half
    for side in range(2):
        out_ref[:, side * cols : side * cols + cols] = buf[low + side * half : low + (side + 1) * half, :]


def last_end(here, bands, bits, half):
    rows = sum(2 * b[0].shape[0] for b in bands)
    cols = bands[0][0].shape[1]
    return call(
        functools.partial(last_end_kernel, bits), "last_end", (1,), [here], [(q, None, None) for b in bands for q in b],
        [((3, 2 * cols, cols), f32, None, None), ((16, cols), f32, None, None), ((half, 2 * cols), f32, None, None)],
        [pltpu.VMEM((rows, cols), f32)],
        free=True,
    )


def contrast(pooled_all, pool_w, pool_bias, log_temp, pairs_all):
    squash_float = jnp.tanh(dot_nn(pooled_all, pool_w) + pool_bias)
    squash = squash_float.astype(bf16).astype(f32)
    inv_norm = lax.rsqrt(jnp.sum(squash * squash, axis=-1, keepdims=True) + 1e-06)
    unit_all = squash * inv_norm
    temp = jnp.exp(-log_temp[0])
    logits = jnp.dot(unit_all, unit_all.T, precision=highest) * temp
    ids = jnp.arange(pooled_all.shape[0], dtype=jnp.int32)
    masked = jnp.where(ids[None, :] == ids[:, None], -1e30, logits)
    row_top = jnp.max(masked, axis=-1, keepdims=True)
    row_expo = jnp.exp(masked - row_top)
    row_total = jnp.sum(row_expo, axis=-1, keepdims=True)
    chosen = (ids[None, :] == pairs_all[:, None]).astype(f32)
    row_lse = row_top[:, 0] + jnp.log(row_total[:, 0])
    loss_total = jnp.sum(row_lse - jnp.sum(chosen * logits, axis=-1))
    grad_logits = row_expo / row_total - chosen
    grad_temp = -jnp.sum(grad_logits * logits)
    grad_unit = jnp.dot(grad_logits + grad_logits.T, unit_all, precision=highest) * temp
    grad_squash = inv_norm * (
        grad_unit - unit_all * jnp.sum(unit_all * grad_unit, axis=-1, keepdims=True)
    )
    grad_pool_pre = (grad_squash * (1.0 - squash_float * squash_float)).astype(bf16)
    return loss_total, grad_temp, grad_pool_pre


def contrast_kernel(
    count, rank_ref, me_ref, all_here, all_there, w_here, w_there, bias_ref, temp_ref, gw_ref, gb_ref,
    gp_ref, scalars_ref, all_ref, w_ref, pooled_ref, grad_ref,
):
    batch, width = pooled_ref.shape
    half = w_here.shape[0]
    me = me_ref[0]
    w_ref[pl.ds(pl.multiple_of(me * half, 128), half), :] = w_here[...]
    w_ref[pl.ds(pl.multiple_of((1 - me) * half, 128), half), :] = w_there[...]
    block = all_here.shape[0]
    rows_all = all_ref.shape[0]
    place(all_ref, me, (all_here, all_there), 0)
    at = lax.broadcasted_iota(jnp.int32, (batch, rows_all), 1)
    row = lax.broadcasted_iota(jnp.int32, (batch, rows_all), 0)
    base = (row // count % 2) * block + (row // count // 2) * 16
    pooled = dot_nn((at == base + row % count).astype(bf16), all_ref[...]).astype(bf16)
    pooled_ref[...] = pooled
    upper = dot_nn((at == base + count).astype(bf16), all_ref[:, :128])
    lower = dot_nn((at == base + count + 1).astype(bf16), all_ref[:, :128])
    lane = lax.broadcasted_iota(jnp.int32, (batch, 128), 1)
    line = lax.broadcasted_iota(jnp.int32, (batch, 128), 0)
    partner = jnp.sum(jnp.where(lane == line % count, upper * 64.0 + lower, 0.0), axis=1, keepdims=True)
    squash_float = jnp.tanh(dot_nn(pooled, w_ref[...]) + bias_ref[...])
    squash = squash_float.astype(bf16).astype(f32)
    inv_norm = lax.rsqrt(jnp.sum(squash * squash, axis=-1, keepdims=True) + 1e-06)
    unit = squash * inv_norm
    temp = jnp.exp(-temp_ref[0:1, 0:1])
    logits = dot_nt(unit, unit, precision=highest) * temp
    ids = lax.broadcasted_iota(jnp.int32, (batch, batch), 1)
    masked = jnp.where(ids == lax.broadcasted_iota(jnp.int32, (batch, batch), 0), -1e30, logits)
    row_top = jnp.max(masked, axis=-1, keepdims=True)
    row_expo = jnp.exp(masked - row_top)
    row_total = jnp.sum(row_expo, axis=-1, keepdims=True)
    chosen = (ids.astype(f32) == partner).astype(f32)
    row_loss = row_top + jnp.log(row_total) - jnp.sum(chosen * logits, axis=-1, keepdims=True)
    loss = jnp.sum(row_loss, axis=0, keepdims=True) / batch
    grad_logits = row_expo / row_total - chosen
    grad_temp = -jnp.sum(jnp.sum(grad_logits * logits, axis=-1, keepdims=True), axis=0, keepdims=True)
    grad_unit = jnp.dot(
        grad_logits + grad_logits.T, unit, precision=highest, preferred_element_type=f32
    ) * temp
    grad_squash = inv_norm * (grad_unit - unit * jnp.sum(unit * grad_unit, axis=-1, keepdims=True))
    grad_pre = (grad_squash * (1.0 - squash_float * squash_float)).astype(bf16)
    gw_ref[...] = dot_tn(pooled_ref[:, lanes_of(me, half)], grad_pre)
    gb_ref[...] = jnp.sum(grad_pre.astype(f32), axis=0, keepdims=True)
    grad_ref[...] = grad_pre.astype(f32)
    own = grad_ref[pl.ds(pl.multiple_of(rank_ref[0] * count, 8), count), :].astype(bf16)
    gp_ref[...] = dot_nt(own, w_ref[...])
    spot = lax.broadcasted_iota(jnp.int32, (8, 128), 1)
    scalars_ref[...] = jnp.where(spot == 0, loss, grad_temp)


def contrast_call(rank, me, gathered, w_here, w_there, bias, log_temp, count):
    width = w_here.shape[1]
    rows_all = 2 * gathered[0].shape[0]
    batch = rows_all // 16 * count
    half = w_here.shape[0]
    temp = jnp.broadcast_to(log_temp.reshape(1, 1), (8, 128))
    return call(
        functools.partial(contrast_kernel, count), "contrast", (1,), [rank, me],
        [(a, None, None) for a in (*gathered, w_here, w_there, bias.reshape(1, width), temp)],
        [
            ((half, width), f32, None, None),
            ((1, width), f32, None, None),
            ((count, width), f32, None, None),
            ((8, 128), f32, None, None),
        ],
        [
            pltpu.VMEM((rows_all, width), bf16),
            pltpu.VMEM((width, width), bf16),
            pltpu.VMEM((batch, width), bf16),
            pltpu.VMEM((batch, width), f32),
        ],
    )


def per_device(
    dp_size,
    tokens,
    qkv_weight,
    qv_bias,
    out_weight,
    out_bias,
    first_gain,
    first_shift,
    up_weight,
    up_bias,
    down_weight,
    down_bias,
    second_gain,
    second_shift,
    pool_weight,
    pool_bias,
    log_temp,
    segments,
    cls_pos,
    pair_index,
    attn_keep,
    ffn_keep,
    grad_out,
):
    me = lax.axis_index("tensor")
    here = lax.axis_index("dp")
    length = segments.shape[1]
    half = tokens.shape[1]
    units = up_bias.shape[0]
    me_one = me.reshape(1).astype(jnp.int32)
    ORDER.clear()
    here_one = here.reshape(1).astype(jnp.int32)
    spot = here_one & 3

    def ordered(mine, theirs, axis):
        return jnp.where(
            me == 0,
            jnp.concatenate([mine, theirs], axis),
            jnp.concatenate([theirs, mine], axis),
        )

    x_there = other(their_rows(me_one, [tokens], length)[0])
    qkv_there = other(qkv_weight)
    vec = jnp.concatenate(
        [qv_bias.reshape(-1), up_bias, out_bias, first_gain, first_shift, down_bias, second_gain, second_shift]
    ).reshape(1, -1)
    out_there = other(out_weight)
    up_there = other(up_weight)
    down_there = other(down_weight)
    pool_there = other(pool_weight)

    seg = lax.dynamic_slice_in_dim(segments, me, 1, 0)
    col = jnp.broadcast_to(seg.reshape(length, 1), (length, 128))
    cls = lax.dynamic_slice_in_dim(cls_pos, me, 1, 0).reshape(-1)
    qv_full, up_b, feats = vectors(me_one, vec, other(vec), units, half)

    x, q, k, v = project(me_one, tokens, x_there, qkv_weight, qkv_there, qv_full, length)
    sends = their_rows(me_one, [attn_keep, ffn_keep], length)
    keep1 = (attn_keep, other(sends[0]))
    keep2 = (ffn_keep, other(sends[1]))
    ctx, lse = attend(seg, col, q, k, v, [])
    res, low, act, slope, mixed, lay_mine, lay_theirs, pooled = feed_forward(
        me_one, cls, pair_index, ctx, x, out_weight, out_there, keep1, up_weight, up_there, down_weight, down_there,
        up_b, feats, keep2,
    )
    quick = dp_size == 16
    if quick:
        near = [pooled] + [across(pooled, m, dp_size) for m in (1, 2, 3)]
    go_there = other(their_rows(me_one, [grad_out], length)[0])
    if quick:
        (near,) = stage(here_one, ("join", near, 0))
        (all_here,) = stage(here_one, ("join", [near] + [across(near, m, dp_size) for m in (4, 8, 12)], 2))
        all_there = other(all_here)
    pool_rows = cls.shape[0]
    rank = here * 2 + me
    batch = dp_size * 2 * pool_rows
    if quick:
        grad_pool_w, grad_pool_b, grad_pooled, scalars = contrast_call(
            rank.reshape(1), me_one, [all_here, all_there], pool_weight, pool_there,
            pool_bias, log_temp, pool_rows,
        )
        grad_pool_b = grad_pool_b.reshape(-1)
        loss, grad_temp = scalars[0, 0], scalars[0, 1]
    else:
        gathered = lax.all_gather(pooled, ("dp", "tensor"), axis=0, tiled=True)
        pool_w = ordered(pool_weight, pool_there, 0)
        gathered = gathered.reshape(-1, pooled.shape[0], D)
        pooled_all = gathered[:, :pool_rows].reshape(-1, D)
        numbers = gathered[:, pool_rows : pool_rows + 2, :pool_rows].astype(jnp.int32)
        pairs_all = (numbers[:, 0] * 64 + numbers[:, 1]).reshape(-1)
        loss_total, grad_temp, grad_pool_pre = contrast(pooled_all, pool_w, pool_bias, log_temp, pairs_all)
        loss = loss_total / batch
        pooled_half = lax.dynamic_slice_in_dim(pooled_all, me * half, half, 1)
        grad_pool_w = dot_tn(pooled_half, grad_pool_pre)
        grad_pool_b = jnp.sum(grad_pool_pre, axis=0, dtype=f32)
        grad_pooled = dot_nt(lax.dynamic_slice_in_dim(grad_pool_pre, rank * pool_rows, pool_rows, 0), pool_w)

    layer_out = both_rows(me_one, lay_mine, other(lay_theirs))
    g, gm, sums2, gd_there = down_back(
        me_one, cls, mixed, grad_out, go_there, grad_pooled, feats, keep2, act
    )
    bit0, bit1 = here_one & 1, (here_one >> 1) & 1
    part, bias_there, gu_there = up_back(bit1, low, g, slope, up_there, down_there, False)
    down = down_own(bit0, act, g, other(gd_there))
    if quick:
        down = Chain(down, (0, 2, 3, 1), dp_size)
    part, bias_here, *up = up_back(bit1, low, g, slope, up_weight, down_weight, True, part, other(gu_there))
    if quick:
        up = Chain(up, (1, 0, 2, 3), dp_size)
    gr, grad_ctx, delta, sums1, go_there, go_here = out_back(
        me_one, gm, part, res, ctx, keep1, out_weight, out_there, feats, []
    )
    go_got = other(go_there)
    if quick:
        advance(here_one, down)
    grads = attend_back(seg, col, q, k, v, grad_ctx, lse, delta, tuple(range(D // PAIR)), [])
    if quick:
        advance(here_one, down, up)
    gq_there, gq_here = qkv_last(me_one, x, grads, bias_here, bias_there, sums1, sums2)
    rows = gq_here.shape[0] + D
    cuts = ((rows // 256 * 128, 0), (rows, 1))
    last = last_halves(here_one, gq_here, other(gq_there), go_here, go_got, cuts)
    if quick:
        orders = ((0, 1, 2, 3), (1, 0, 2, 3))
        last = [Chain(halves, order, dp_size) for halves, order in zip(last, orders)]
    gt_mine, gt_theirs = tokens_back(me_one, gr, grads, qkv_weight, qkv_there)
    if quick:
        while any(chain.step < 7 for chain in (down, up, *last)):
            for chain in (*last, down, up):
                if chain.step < 7:
                    advance(here_one, chain, free=True)
        down, up = down.parts, up.parts
        last = [chain.parts for chain in last]
    else:
        down, up = plain_sum(bit0[0], down), plain_sum(bit1[0], up)
        last = [plain_sum((here >> bit) & 1, halves) for halves, (_, bit) in zip(last, cuts)]
    grad_tokens = both_rows(me_one, gt_mine, other(gt_theirs))
    g_down_w = end(bit0, down, "down_end")
    g_up_w = end(bit1, up, "up_end")
    g_qkv_w, vec_sum, g_out_w = last_end(here_one, last, (0, 1), half)
    n_up = units // half
    return (
        layer_out,
        loss.reshape(1),
        grad_tokens,
        g_qkv_w,
        vec_sum[:2],
        g_out_w,
        vec_sum[2 + n_up],
        vec_sum[3 + n_up],
        vec_sum[4 + n_up],
        g_up_w,
        vec_sum[2 : 2 + n_up].reshape(-1),
        g_down_w,
        vec_sum[5 + n_up],
        vec_sum[6 + n_up],
        vec_sum[7 + n_up],
        grad_pool_w,
        grad_pool_b,
        grad_temp.reshape(1),
    )


def solution(mesh):
    return jax.shard_map(
        functools.partial(per_device, mesh.shape["dp"]),
        mesh=mesh,
        in_specs=(
            P("dp", "tensor"),
            P(None, None, "tensor"),
            P(None, "tensor"),
            P("tensor", None),
            P("tensor"),
            P("tensor"),
            P("tensor"),
            P(None, "tensor"),
            P("tensor"),
            P("tensor", None),
            P("tensor"),
            P("tensor"),
            P("tensor"),
            P("tensor", None),
            P(),
            P(),
            P("dp", None),
            P("dp", None),
            P("dp"),
            P("dp", "tensor"),
            P("dp", "tensor"),
            P("dp", "tensor"),
        ),
        out_specs=(
            P("dp", "tensor"),
            P(),
            P("dp", "tensor"),
            P(None, None, "tensor"),
            P(None, "tensor"),
            P("tensor", None),
            P("tensor"),
            P("tensor"),
            P("tensor"),
            P(None, "tensor"),
            P("tensor"),
            P("tensor", None),
            P("tensor"),
            P("tensor"),
            P("tensor"),
            P("tensor", None),
            P(),
            P(),
        ),
        check_vma=False,
    )
```

```python
import functools
import jax
import jax.numpy as jnp
from jax import lax
from jax.experimental import pallas as pl
from jax.experimental.pallas import tpu as pltpu
from jax.sharding import PartitionSpec as P

D = 768
HEAD_DIM = 64
PAIR = 2 * HEAD_DIM
BLOCK = 256
QROWS = 128
WIDE = QROWS + 512
NEAR = QROWS + 256
SWAP = [(0, 1), (1, 0)]
highest = lax.Precision.HIGHEST
f32 = jnp.float32
bf16 = jnp.bfloat16


def dot_nt(a, b, **kw):
    return lax.dot_general(a, b, (((1,), (1,)), ((), ())), preferred_element_type=f32, **kw)


def dot_tn(a, b):
    return lax.dot_general(a, b, (((0,), (0,)), ((), ())), preferred_element_type=f32)


def dot_nn(a, b):
    return jnp.dot(a, b, preferred_element_type=f32)


ORDER = []

VMEM = {
    "their_rows": 6, "both_rows": 10, "vectors": 4, "qkv": 20, "attend": 18, "contrast": 20, "down_own": 20,
    "last_halves": 20, "stage": 18, "up_end": 12, "down_end": 12, "last_end": 20, "attend_back": 24, "qkv_last": 24,
}

MICROS = {
    "their_rows": 2, "both_rows": 2, "vectors": 1, "qkv": 5, "pooled": 9, "attend": 11, "ffn": 25, "contrast": 6, "down_back": 9,
    "down_own": 3.5, "up_back": 10, "up_own": 10, "out_back": 9, "attend_back": 21, "qkv_last": 4,
    "tokens_back": 5, "last_halves": 2, "stage": 1, "up_end": 3, "last_end": 3, "down_end": 3,
}


def norm(v):
    center = v - jnp.mean(v, axis=-1, keepdims=True)
    inv = lax.rsqrt(jnp.mean(center * center, axis=-1, keepdims=True) + 1e-06)
    return center * inv, inv


def norm_back(upstream, unit, inv, gain):
    scaled = upstream * gain
    return inv * (
        scaled
        - jnp.mean(scaled, axis=-1, keepdims=True)
        - unit * jnp.mean(scaled * unit, axis=-1, keepdims=True)
    )


def gelu_both(x):
    phi = 0.5 * (1.0 + lax.erf(x * (0.5 ** 0.5)))
    bell = jnp.exp(-0.5 * x * x) * 0.3989422804014327
    return x * phi, phi + x * bell


def lanes_of(me, half):
    return pl.ds(pl.multiple_of(me * half, 128), half)


def call(kernel, name, grid, scalars, ins, outs, scratch=(), vmem=26, after=(), aliases=None, free=False):
    after = [*after, *([] if free else ORDER[-1:])]
    n_scalars, n_ins, n_after = len(scalars), len(ins), len(after)

    def body(*refs):
        cut = n_scalars + n_ins
        kernel(*refs[:cut], *refs[cut + n_after :])

    def spec(shape, block, index):
        if block is None:
            zeros = (0,) * len(shape)
            return pl.BlockSpec(shape, lambda *a: zeros)
        return pl.BlockSpec(block, index)

    arrays = [a if b is None else pltpu.with_memory_space_constraint(a, pltpu.HBM) for a, b, _ in ins]
    result = pl.pallas_call(
        body,
        grid_spec=pltpu.PrefetchScalarGridSpec(
            num_scalar_prefetch=len(scalars),
            grid=grid,
            in_specs=[spec(a.shape, b, i) for a, b, i in ins]
            + [pl.BlockSpec(memory_space=pl.ANY)] * n_after,
            out_specs=[spec(s, b, i) for s, _, b, i in outs],
            scratch_shapes=list(scratch),
        ),
        out_shape=[jax.ShapeDtypeStruct(s, d) for s, d, _, _ in outs],
        compiler_params=pltpu.CompilerParams(vmem_limit_bytes=VMEM.get(name, vmem) << 20),
        cost_estimate=pl.CostEstimate(flops=int(MICROS[name] * 1.15e9), bytes_accessed=1000, transcendentals=0),
        input_output_aliases={n_scalars + i: o for i, o in (aliases or {}).items()},
        name=name,
    )(*scalars, *arrays, *after)
    if not free:
        ORDER.append(min(result, key=lambda r: r.size))
    return result


def put_halves(buf, me, mine, theirs):
    half = mine.shape[1]
    buf[:, lanes_of(me, half)] = mine.astype(buf.dtype)
    buf[:, lanes_of(1 - me, half)] = theirs.astype(buf.dtype)


def rows_kernel(me_ref, *refs):
    for i, o in zip(refs[: len(refs) // 2], refs[len(refs) // 2 :]):
        o[...] = i[...].astype(bf16)


def their_rows(me, arrays, length, after=()):
    half = arrays[0].shape[1]
    steps = length // 256
    return call(
        rows_kernel, "their_rows", (steps,), [me],
        [(a, (256, half), lambda i, m: ((1 - m[0]) * steps + i, 0)) for a in arrays],
        [((length, half), bf16, (256, half), lambda i, m: (i, 0))] * len(arrays),
        after=after,
    )


def both_rows_kernel(me_ref, mine, theirs, out):
    own = pl.program_id(0) // 2 == me_ref[0]

    @pl.when(own)
    def _():
        out[...] = mine[...]

    @pl.when(jnp.logical_not(own))
    def _():
        out[...] = theirs[...]


def both_rows(me, mine, theirs):
    length, half = mine.shape
    block = (length // 2, half)
    turn = lambda i, m: (i % 2, 0)
    return call(
        both_rows_kernel, "both_rows", (4,), [me], [(mine, block, turn), (theirs, block, turn)],
        [((2 * length, half), mine.dtype, block, lambda i, m: (i, 0))],
        free=True,
    )[0]


def vectors_kernel(units, me_ref, mine, theirs, qv_ref, up_ref, feats_ref):
    half = qv_ref.shape[1] // 2
    feats_ref[...] = jnp.zeros_like(feats_ref)
    for side, vec in enumerate((mine, theirs)):
        for row in range(2):
            qv_ref[row : row + 1, side * half : side * half + half] = vec[:, row * half : row * half + half]
        up_ref[:, side * units : side * units + units] = vec[:, 2 * half : 2 * half + units]
        spot = lanes_of(me_ref[0] if side == 0 else 1 - me_ref[0], half)
        for row in range(6):
            low = 2 * half + units + row * half
            feats_ref[row : row + 1, spot] = vec[:, low : low + half]


def vectors(me, mine, theirs, units, half):
    return call(
        functools.partial(vectors_kernel, units), "vectors", (1,), [me],
        [(mine, None, None), (theirs, None, None)],
        [((2, 2 * half), f32, None, None), ((1, 2 * units), f32, None, None), ((8, 2 * half), f32, None, None)],
    )


def qkv_kernel(me_ref, mine, theirs, w_here, w_there, bias, x_ref, q_ref, k_ref, v_ref):
    put_halves(x_ref, me_ref[0], mine[...], theirs[...])
    half = mine.shape[1]
    for c, out in enumerate((q_ref, k_ref, v_ref)):
        for side, w in enumerate((w_here, w_there)):
            cols = slice(side * half, side * half + half)
            y = dot_nn(x_ref[...], w[c])
            if c != 1:
                y = y + bias[c // 2 : c // 2 + 1, cols]
            out[:, cols] = y.astype(bf16)


def project(me, tokens, x_there, w_here, w_there, bias, length):
    half = tokens.shape[1]
    rows = 512
    steps = length // rows
    band = (rows, 2 * half)
    return call(
        qkv_kernel, "qkv", (steps,), [me],
        [
            (tokens, (rows, half), lambda i, m: (m[0] * steps + i, 0)),
            (x_there, (rows, half), lambda i, m: (i, 0)),
            (w_here, None, None),
            (w_there, None, None),
            (bias, None, None),
        ],
        [((length, 2 * half), bf16, band, lambda i, m: (i, 0))] * 4,
    )


def window_paths(step, length, seg_ref, run):
    first = step * QROWS
    near = pl.multiple_of(jnp.clip(first - 128, 0, length - NEAR), 128)
    left = seg_ref[jnp.maximum(near - 1, 0)] == seg_ref[first]
    right = seg_ref[jnp.minimum(near + NEAR, length - 1)] == seg_ref[first + QROWS - 1]
    spills = jnp.logical_or(
        jnp.logical_and(near > 0, left), jnp.logical_and(near + NEAR < length, right)
    )
    far = pl.multiple_of(jnp.clip(first - 256, 0, length - WIDE), 128)

    @pl.when(jnp.logical_not(spills))
    def _():
        run(NEAR, near)

    @pl.when(spills)
    def _():
        run(WIDE, far)


def fill_bias(bias_ref, col_ref, row_ref, width, start):
    bias = jnp.where(col_ref[pl.ds(start, width), :] == row_ref[...], 0.0, -1e30)
    for n in range(bias_ref.shape[1] // QROWS):
        bias_ref[0:width, n * QROWS : (n + 1) * QROWS] = bias


def head_mask(h):
    lane = lax.broadcasted_iota(jnp.int32, (1, PAIR), 1)
    return (lane // HEAD_DIM == h).astype(bf16)


def attend_kernel(length, pairs, seg_ref, col_ref, row_ref, q_ref, k_ref, v_ref, ctx_ref, lse_ref, bias_ref):
    def run(width, start):
        fill_bias(bias_ref, col_ref, row_ref, width, start)
        rows = pl.ds(start, width)
        for j in range(pairs):
            lanes = slice(j * PAIR, j * PAIR + PAIR)
            q2 = q_ref[:, lanes] * bf16(HEAD_DIM ** (-0.5))
            keys = k_ref[rows, lanes]
            values = v_ref[rows, lanes]
            parts = []
            for h in range(2):
                scores = dot_nt(keys, q2 * head_mask(h)) + bias_ref[0:width, :]
                top = jnp.max(scores, axis=0, keepdims=True)
                expo = jnp.exp(scores - top)
                total = jnp.sum(expo, axis=0, keepdims=True)
                out = dot_tn(values, expo.astype(bf16))[h * HEAD_DIM : (h + 1) * HEAD_DIM]
                parts.append(out * (1.0 / total))
                lse_ref[8 * h + j : 8 * h + j + 1, :] = top + jnp.log(total)
            ctx_ref[:, lanes] = jnp.concatenate(parts, axis=0).T.astype(bf16)

    window_paths(pl.program_id(0), length, seg_ref, run)


def attend(seg, col, q, k, v, after):
    length, width = q.shape
    band = lambda i, s: (i, 0)
    block = (QROWS, width)
    return call(
        functools.partial(attend_kernel, length, width // PAIR), "attend", (length // QROWS,),
        [seg.reshape(length)],
        [
            (col, None, None),
            (seg.reshape(1, length), (1, QROWS), lambda i, s: (0, i)),
            (q, block, band),
            (k, None, None),
            (v, None, None),
        ],
        [
            ((length, width), bf16, block, band),
            ((16, length), f32, (16, QROWS), lambda i, s: (0, i)),
        ],
        [pltpu.VMEM((WIDE, QROWS), f32)],
        after=after,
    )


def attend_back_kernel(
    length, chosen, seg_ref, col_ref, row_ref, q_ref, k_ref, v_ref, do_ref, lse_ref, delta_ref,
    dq_ref, dk_ref, dv_ref, bias_ref, dk_acc, dv_acc,
):
    step = pl.program_id(0)

    @pl.when(step == 0)
    def _():
        dk_acc[...] = jnp.zeros_like(dk_acc)
        dv_acc[...] = jnp.zeros_like(dv_acc)

    def both(ref, j):
        return jnp.concatenate([ref[j : j + 1, :], ref[8 + j : 9 + j, :]], axis=1)

    def run(width, start):
        fill_bias(bias_ref, col_ref, row_ref, width, start)
        rows = pl.ds(start, width)
        for n, j in enumerate(chosen):
            lanes = slice(j * PAIR, j * PAIR + PAIR)
            slot = slice(n * PAIR, n * PAIR + PAIR)
            q2 = q_ref[:, lanes] * bf16(HEAD_DIM ** (-0.5))
            do2 = do_ref[:, lanes]
            keys = k_ref[rows, lanes]
            values = v_ref[rows, lanes]
            queries = jnp.concatenate([q2 * head_mask(0), q2 * head_mask(1)], axis=0)
            grads = jnp.concatenate([do2 * head_mask(0), do2 * head_mask(1)], axis=0)
            scores = dot_nt(keys, queries) + bias_ref[0:width, :]
            probs = jnp.exp(scores - both(lse_ref, j))
            grad_probs = dot_nt(values, grads)
            grad_scores = (probs * (grad_probs - both(delta_ref, j))).astype(bf16)
            dv_acc[rows, slot] += dot_nn(probs.astype(bf16), grads)
            dk_acc[rows, slot] += dot_nn(grad_scores, queries)
            dq = dot_tn(keys, grad_scores)
            dq = jnp.concatenate([dq[:HEAD_DIM, :QROWS], dq[HEAD_DIM:, QROWS:]], axis=0).T
            dq_ref[:, slot] = (dq * (HEAD_DIM ** (-0.5))).astype(bf16)

    window_paths(step, length, seg_ref, run)

    @pl.when(step == length // QROWS - 1)
    def _():
        dk_ref[...] = dk_acc[...].astype(bf16)
        dv_ref[...] = dv_acc[...].astype(bf16)


def attend_back(seg, col, q, k, v, grad_ctx, lse, delta, chosen, after):
    length, width = q.shape
    cols = len(chosen) * PAIR
    block = (QROWS, width)
    band = lambda i, s: (i, 0)
    flat = lambda i, s: (0, i)
    whole = ((length, cols), bf16, None, None)
    return call(
        functools.partial(attend_back_kernel, length, chosen), "attend_back", (length // QROWS,),
        [seg.reshape(length)],
        [
            (col, None, None),
            (seg.reshape(1, length), (1, QROWS), flat),
            (q, block, band),
            (k, None, None),
            (v, None, None),
            (grad_ctx, block, band),
            (lse, (16, QROWS), flat),
            (delta, (16, QROWS), flat),
        ],
        [((length, cols), bf16, (QROWS, cols), band), whole, whole],
        [
            pltpu.VMEM((WIDE, 2 * QROWS), f32),
            pltpu.VMEM((length, cols), f32),
            pltpu.VMEM((length, cols), f32),
        ],
        after=after,
    )


UNITS = 512
FROWS = 512


def sides(sides_count, step, here_first, run_here, run_there):
    low, high = (run_here, run_there) if here_first else (run_there, run_here)

    @pl.when(step < sides_count)
    def _():
        low()

    @pl.when(step >= sides_count)
    def _():
        high()


def ffn_kernel(
    count, me_ref, cls_ref, pair_ref, ctx_ref, x_ref, ow_here, ow_there, keep1_mine, keep1_theirs, uw_here, uw_there, dw_here,
    dw_there, up_b, feats, keep_mine, keep_theirs, res_ref, low_ref, act_ref, slope_ref, mixed_ref, mine_ref,
    theirs_ref, pooled_ref, keep, keep2, value_buf,
):
    step = pl.program_id(0)
    length = low_ref.shape[0]

    @pl.when(step == 0)
    def _():
        mixed_ref[...] = jnp.zeros_like(mixed_ref)
        side = ow_here.shape[0]
        for r in range(length // BLOCK):
            rows = slice(r * BLOCK, (r + 1) * BLOCK)
            put_halves(keep, me_ref[0], keep1_mine[rows, :].astype(f32), keep1_theirs[rows, :])
            branch = dot_nn(ctx_ref[rows, :side], ow_here[...]) + dot_nn(ctx_ref[rows, side:], ow_there[...])
            residual = x_ref[rows, :].astype(f32) + (branch + feats[0:1, :]) * (keep[...] * (1 / 0.9))
            res_ref[rows, :] = residual
            low_ref[rows, :] = (norm(residual)[0] * feats[1:2, :] + feats[2:3, :]).astype(bf16)

    @pl.when(step < length // BLOCK)
    def _():
        rows = pl.ds(pl.multiple_of(step * BLOCK, BLOCK), BLOCK)
        put_halves(keep2.at[rows, :], me_ref[0], keep_mine[...], keep_theirs[...])

    def run(up, down):
        def go():
            for r in range(length // FROWS):
                rows = slice(r * FROWS, (r + 1) * FROWS)
                pre = dot_nn(low_ref[rows, :], up[...]) + up_b[...]
                value, slope = gelu_both(pre)
                value = value.astype(bf16)
                act_ref[rows, :] = value
                slope_ref[rows, :] = slope.astype(bf16)
                mixed_ref[rows, :] += dot_nn(value, down[...])

        return go

    sides(count, step, True, run(uw_here, dw_here), run(uw_there, dw_there))

    @pl.when(step == 2 * count - 1)
    def _():
        half = mine_ref.shape[1]
        me = me_ref[0]
        width = value_buf.shape[1]
        chosen = cls_ref.shape[0]
        line = lax.broadcasted_iota(jnp.int32, (16, BLOCK), 0)
        spot = jnp.full((16, BLOCK), -1, jnp.int32)
        for c in range(chosen):
            spot = jnp.where(line == c, cls_ref[c], spot)
        line = lax.broadcasted_iota(jnp.int32, (16, width), 0)
        lane = lax.broadcasted_iota(jnp.int32, (16, width), 1)
        numbers = jnp.zeros((16, width), jnp.int32)
        for c in range(chosen):
            number = pair_ref[me * chosen + c]
            numbers = jnp.where((lane == c) & (line == chosen), number // 64, numbers)
            numbers = jnp.where((lane == c) & (line == chosen + 1), number % 64, numbers)
        pooled = numbers.astype(f32)
        for r in range(length // BLOCK):
            rows = slice(r * BLOCK, (r + 1) * BLOCK)
            hidden = norm(res_ref[rows, :])[0] * feats[1:2, :] + feats[2:3, :]
            mixed = hidden + (mixed_ref[rows, :] + feats[3:4, :]) * (keep2[rows, :].astype(f32) * (1 / 0.9))
            mixed_ref[rows, :] = mixed
            value_buf[...] = (norm(mixed)[0] * feats[4:5, :] + feats[5:6, :]).astype(bf16)
            here = lax.broadcasted_iota(jnp.int32, (16, BLOCK), 1) + r * BLOCK
            pooled = pooled + dot_nn((here == spot).astype(bf16), value_buf[...])
            mine_ref[rows, :] = value_buf[:, lanes_of(me, half)]
            theirs_ref[rows, :] = value_buf[:, lanes_of(1 - me, half)]
        pooled_ref[...] = pooled.astype(bf16)


def feed_forward(me, cls, pair_index, ctx, x, ow_here, ow_there, keep1, uw_here, uw_there, dw_here, dw_there, up_b, feats, keep):
    length, width = x.shape
    half = width // 2
    count = uw_here.shape[1] // UNITS
    units = 2 * uw_here.shape[1]
    bands = length // BLOCK
    assert bands <= 2 * count
    first = lambda i: jnp.minimum(i, count - 1)
    second = lambda i: jnp.maximum(i - count, 0)
    return call(
        functools.partial(ffn_kernel, count), "ffn", (2 * count,), [me, cls, pair_index],
        [
            (ctx, None, None),
            (x, None, None),
            (ow_here, None, None),
            (ow_there, None, None),
            (keep1[0], (length, half), lambda i, m, c, p: (m[0], 0)),
            (keep1[1], None, None),
            (uw_here, (width, UNITS), lambda i, m, c, p: (0, first(i))),
            (uw_there, (width, UNITS), lambda i, m, c, p: (0, second(i))),
            (dw_here, (UNITS, width), lambda i, m, c, p: (first(i), 0)),
            (dw_there, (UNITS, width), lambda i, m, c, p: (second(i), 0)),
            (up_b, (1, UNITS), lambda i, m, c, p: (0, i)),
            (feats, None, None),
            (keep[0], (BLOCK, half), lambda i, m, c, p: (m[0] * bands + jnp.minimum(i, bands - 1), 0)),
            (keep[1], (BLOCK, half), lambda i, m, c, p: (jnp.minimum(i, bands - 1), 0)),
        ],
        [
            ((length, width), f32, None, None),
            ((length, width), bf16, None, None),
            ((length, units), bf16, (length, UNITS), lambda i, m, c, p: (0, i)),
            ((length, units), bf16, (length, UNITS), lambda i, m, c, p: (0, i)),
            ((length, width), f32, None, None),
            ((length, half), bf16, None, None),
            ((length, half), bf16, None, None),
            ((16, width), bf16, None, None),
        ],
        [pltpu.VMEM((BLOCK, width), f32), pltpu.VMEM((length, width), bf16), pltpu.VMEM((BLOCK, width), bf16)],
        vmem=36,
    )


def down_back_kernel(
    me_ref, cls_ref, mixed_ref, go_mine, go_theirs, pooled_ref, feats, keep_mine, keep_theirs, act_ref,
    g_ref, gm_ref, sums_ref, there_ref, buf, keep,
):
    length, width = mixed_ref.shape

    @pl.when(pl.program_id(0) == 0)
    def _():
        me = me_ref[0]
        put_halves(buf, me, go_mine[...].astype(f32), go_theirs[...])
        for c in range(cls_ref.shape[0]):
            spot = pl.ds(cls_ref[c], 1)
            buf[spot, :] = buf[spot, :] + pooled_ref[c : c + 1, :]
        gain_sum = jnp.zeros((1, width), f32)
        shift_sum = jnp.zeros((1, width), f32)
        bias_sum = jnp.zeros((1, width), f32)
        for r in range(length // BLOCK):
            rows = slice(r * BLOCK, (r + 1) * BLOCK)
            upstream = buf[rows, :]
            unit, inv = norm(mixed_ref[rows, :])
            back = norm_back(upstream, unit, inv, feats[4:5, :])
            gm_ref[rows, :] = back
            put_halves(keep, me, keep_mine[rows, :].astype(f32), keep_theirs[rows, :])
            g = (back * (keep[...] * (1 / 0.9))).astype(bf16)
            g_ref[rows, :] = g
            gain_sum = gain_sum + jnp.sum(upstream * unit, axis=0, keepdims=True)
            shift_sum = shift_sum + jnp.sum(upstream, axis=0, keepdims=True)
            bias_sum = bias_sum + jnp.sum(g.astype(f32), axis=0, keepdims=True)
        sums_ref[...] = jnp.concatenate(
            [bias_sum, gain_sum, shift_sum, jnp.zeros((5, width), f32)], axis=0
        )

    there_ref[...] = dot_tn(act_ref[...], g_ref[...]).astype(bf16)


def down_back(me, cls, mixed, go_arg, go_there, grad_pooled, feats, keep, act):
    length, width = mixed.shape
    half = width // 2
    units = act.shape[1] // 2
    count = units // UNITS
    part = lambda a: (a, (length, half), lambda i, m, c: (m[0], 0))
    return call(
        down_back_kernel, "down_back", (count,), [me, cls],
        [
            (mixed, None, None),
            part(go_arg),
            (go_there, None, None),
            (grad_pooled, None, None),
            (feats, None, None),
            part(keep[0]),
            (keep[1], None, None),
            (act, (length, UNITS), lambda i, m, c: (0, i + count)),
        ],
        [
            ((length, width), bf16, None, None),
            ((length, width), f32, None, None),
            ((8, width), f32, None, None),
            ((units, width), bf16, (UNITS, width), lambda i, m, c: (i, 0)),
        ],
        [pltpu.VMEM((length, width), f32), pltpu.VMEM((BLOCK, width), f32)],
    )


def down_own_kernel(bit_ref, act_ref, g_ref, got_ref, keep_ref, send_ref):
    grad = (dot_tn(act_ref[...], g_ref[...]) + got_ref[...].astype(f32)).astype(bf16)
    mine = pl.program_id(0) == bit_ref[0]

    @pl.when(mine)
    def _():
        keep_ref[...] = grad

    @pl.when(jnp.logical_not(mine))
    def _():
        send_ref[...] = grad


def down_own(bit, act, g, got):
    length, width = g.shape
    rows = got.shape[0] // 2
    return call(
        down_own_kernel, "down_own", (2,), [bit],
        [
            (act, (length, rows), lambda i, s: (0, i)),
            (g, None, None),
            (got, (rows, width), lambda i, s: (i, 0)),
        ],
        [((rows, width), bf16, None, None)] * 2,
    )


def up_back_kernel(
    own, bit_ref, low_ref, g_ref, slope_ref, up, down, *refs,
):
    if own:
        start_ref, got_ref, part_ref, bias_ref, *out_refs, grad_buf = refs
    else:
        part_ref, bias_ref, out_ref = refs
    step = pl.program_id(0)
    length, width = g_ref.shape

    @pl.when(step == 0)
    def _():
        part_ref[...] = start_ref[...] if own else jnp.zeros_like(part_ref)

    total = jnp.zeros((1, UNITS), f32)
    grads = []
    for r in range(length // FROWS):
        rows = slice(r * FROWS, (r + 1) * FROWS)
        gu = (dot_nt(g_ref[rows, :], down[...]) * slope_ref[rows, :].astype(f32)).astype(bf16)
        total = total + jnp.sum(gu.astype(f32), axis=0, keepdims=True)
        part_ref[rows, :] += dot_nt(gu, up[...])
        grads.append(gu)
    bias_ref[...] = total
    grad = dot_tn(low_ref[...], jnp.concatenate(grads, axis=0))
    if own:
        grad_buf[...] = (grad + got_ref[...].astype(f32)).astype(bf16)
        halves_out(bit_ref[0], grad_buf, out_refs)
    else:
        out_ref[...] = grad.astype(bf16)


def up_back(bit, low, g, slope, up, down, own, start=None, got=None, after=()):
    length, width = g.shape
    units = up.shape[1]
    count = units // UNITS
    skip = 0 if own else count
    ins = [
        (low, None, None),
        (g, None, None),
        (slope, (length, UNITS), lambda i, s: (0, i + skip)),
        (up, (width, UNITS), lambda i, s: (0, i)),
        (down, (UNITS, width), lambda i, s: (i, 0)),
    ]
    rows = width // 2 if own else width
    outs = [
        ((length, width), f32, None, None),
        ((1, units), f32, (1, UNITS), lambda i, s: (0, i)),
    ] + [((rows, units), bf16, (rows, UNITS), lambda i, s: (0, i))] * (width // rows)
    scratch = []
    if own:
        scratch = [pltpu.VMEM((width, UNITS), bf16)]
        ins += [(start, None, None), (got, (width, UNITS), lambda i, s: (0, i))]
    return call(
        functools.partial(up_back_kernel, own), "up_own" if own else "up_back", (count,), [bit], ins, outs, scratch,
        after=after,
    )


def out_back_kernel(
    me_ref, gm_ref, part_ref, res_ref, ctx_ref, keep_mine, keep_theirs, w_here, w_there, feats,
    gr_ref, gc_ref, delta_ref, sums_ref, there_ref, here_ref, keep, acc, sums,
):
    step = pl.program_id(0)
    width = gm_ref.shape[1]
    half = width // 2
    rows = pl.ds(pl.multiple_of(step * BLOCK, BLOCK), BLOCK)
    unit, inv = norm(res_ref[rows, :])
    upstream = gm_ref[rows, :] + part_ref[rows, :]
    back = norm_back(upstream, unit, inv, feats[1:2, :])
    gr_ref[...] = back
    put_halves(keep, me_ref[0], keep_mine[...].astype(f32), keep_theirs[...])
    g = (back * (keep[...] * (1 / 0.9))).astype(bf16)
    gc_ref[:, :half] = dot_nt(g, w_here[...]).astype(bf16)
    gc_ref[:, half:] = dot_nt(g, w_there[...]).astype(bf16)
    grad = dot_tn(ctx_ref[...], g)
    prod = gc_ref[...].astype(f32) * ctx_ref[...].astype(f32)
    high = prod.astype(bf16)
    rest = (prod - high.astype(f32)).astype(bf16)
    row = lax.broadcasted_iota(jnp.int32, (16, width), 0)
    lane = lax.broadcasted_iota(jnp.int32, (16, width), 1)
    pick = (lane // HEAD_DIM == (row & 7) * 2 + (row >> 3)).astype(bf16)
    delta_ref[...] = dot_nt(pick, high) + dot_nt(pick, rest)
    parts = [
        jnp.sum(g.astype(f32), axis=0, keepdims=True),
        jnp.sum(upstream * unit, axis=0, keepdims=True),
        jnp.sum(upstream, axis=0, keepdims=True),
        jnp.zeros((5, width), f32),
    ]
    row = jnp.concatenate(parts, axis=0)

    @pl.when(step == 0)
    def _():
        acc[...] = grad
        sums[...] = row

    @pl.when(step > 0)
    def _():
        acc[...] += grad
        sums[...] += row

    @pl.when(step == pl.num_programs(0) - 1)
    def _():
        here_ref[...] = acc[:half, :].astype(bf16)
        there_ref[...] = acc[half:, :].astype(bf16)
        sums_ref[...] = sums[...]


def out_back(me, gm, part, res, ctx, keep, w_here, w_there, feats, after):
    length, width = gm.shape
    half = width // 2
    steps = length // BLOCK
    band = lambda i, m: (i, 0)
    block = (BLOCK, width)
    return call(
        out_back_kernel, "out_back", (steps,), [me],
        [
            (gm, None, None),
            (part, None, None),
            (res, None, None),
            (ctx, block, band),
            (keep[0], (BLOCK, half), lambda i, m: (m[0] * steps + i, 0)),
            (keep[1], (BLOCK, half), band),
            (w_here, None, None),
            (w_there, None, None),
            (feats, None, None),
        ],
        [
            ((length, width), f32, block, band),
            ((length, width), bf16, block, band),
            ((16, length), f32, (16, BLOCK), lambda i, m: (0, i)),
            ((8, width), f32, None, None),
            ((half, width), bf16, None, None),
            ((half, width), bf16, None, None),
        ],
        [pltpu.VMEM((BLOCK, width), f32), pltpu.VMEM((width, width), f32), pltpu.VMEM((8, width), f32)],
        after=after,
    )


def qkv_last_kernel(
    me_ref, x_ref, dq, dk, dv, bias_here, bias_there, sums1, sums2, there_ref, here_ref, vh, vt, both,
):
    width = x_ref.shape[1]
    half = width // 2
    sums = []
    for c, g in enumerate((dq, dk, dv)):
        grad = dot_tn(x_ref[...], g[...]).astype(bf16)
        here_ref[c * width : (c + 1) * width, :] = grad[:, :half]
        there_ref[c * width : (c + 1) * width, :] = grad[:, half:]
        if c != 1:
            sums.append(jnp.sum(g[...].astype(f32), axis=0, keepdims=True))
    vh[...] = jnp.zeros_like(vh)
    vt[...] = jnp.zeros_like(vt)
    for side, (v, bias) in enumerate(((vh, bias_here), (vt, bias_there))):
        for row in range(2):
            v[row : row + 1, :] = sums[row][:, side * half : side * half + half]
        at = 2
        for n in range(bias.shape[1] // half):
            v[at : at + 1, :] = bias[:, n * half : (n + 1) * half]
            at += 1
    both[0:8, :] = sums1[...]
    both[8:16, :] = sums2[...]
    for v, m in ((vh, me_ref[0]), (vt, 1 - me_ref[0])):
        v[at : at + 3, :] = both[0:3, lanes_of(m, half)]
        v[at + 3 : at + 6, :] = both[8:11, lanes_of(m, half)]
    low = 3 * width
    for v, ref in ((vh, here_ref), (vt, there_ref)):
        ref[low : low + 16, :] = v[...].astype(bf16)
        ref[low + 16 :, :] = jnp.zeros((ref.shape[0] - low - 16, half), bf16)


def qkv_last(me, x, grads, bias_here, bias_there, sums1, sums2):
    width = x.shape[1]
    half = width // 2
    return call(
        qkv_last_kernel, "qkv_last", (1,), [me],
        [(a, None, None) for a in (x, *grads, bias_here, bias_there, sums1, sums2)],
        [((3 * width + 128, half), bf16, None, None)] * 2,
        [pltpu.VMEM((16, half), f32), pltpu.VMEM((16, half), f32), pltpu.VMEM((16, width), f32)],
    )


def tokens_back_kernel(me_ref, gr_ref, dq, dk, dv, w_here, w_there, mine_ref, theirs_ref, buf):
    half = mine_ref.shape[1]
    total = gr_ref[...]
    rows = pl.ds(pl.multiple_of(pl.program_id(0) * 512, 512), 512)
    for c, g in enumerate((dq[...], dk[rows, :], dv[rows, :])):
        total = total + dot_nt(g[:, :half], w_here[c]) + dot_nt(g[:, half:], w_there[c])
    buf[...] = total
    mine_ref[...] = buf[:, lanes_of(me_ref[0], half)]
    theirs_ref[...] = buf[:, lanes_of(1 - me_ref[0], half)]


def tokens_back(me, gr, grads, w_here, w_there):
    length, width = gr.shape
    half = width // 2
    band = lambda i, m: (i, 0)
    return call(
        tokens_back_kernel, "tokens_back", (length // 512,), [me],
        [(a, (512, width), band) for a in (gr, grads[0])]
        + [(a, None, None) for a in (*grads[1:], w_here, w_there)],
        [((length, half), f32, (512, half), band)] * 2,
        [pltpu.VMEM((512, width), f32)],
    )


def other(x):
    return lax.ppermute(x, "tensor", SWAP)


def across(x, mask, size):
    return lax.ppermute(x, "dp", [(i, i ^ mask) for i in range(size)])


def halves_out(at, buf, outs, low=0):
    rows = outs[0].shape[0]
    for m, out in enumerate(outs):
        start = pl.multiple_of(low + (at ^ m) * rows, 8)
        out[...] = buf[pl.ds(start, rows), :].astype(bf16)


def last_parts_kernel(bands, here_ref, gq_here, gq_got, go_here, go_got, *refs):
    *outs, buf = refs
    rows, cols = gq_here.shape
    buf[:rows, :] = gq_here[...].astype(f32) + gq_got[...].astype(f32)
    half = go_here.shape[0]
    for side in range(2):
        lanes = slice(side * cols, side * cols + cols)
        low = rows + side * half
        buf[low : low + half, :] = go_here[:, lanes].astype(f32) + go_got[:, lanes].astype(f32)
    low = 0
    for high, (bit, width) in bands:
        many = 1 << width
        halves_out((here_ref[0] >> bit) & (many - 1), buf, outs[:many], low)
        outs = outs[many:]
        low = high


def last_parts(here, gq_here, gq_got, go_here, go_got, bands):
    rows, cols = gq_here.shape
    rows += 2 * go_here.shape[0]
    lows = [0] + [high for high, _ in bands[:-1]]
    sizes = [((high - low) >> width, 1 << width) for low, (high, (_, width)) in zip(lows, bands)]
    outs = call(
        functools.partial(last_parts_kernel, bands), "last_halves", (1,), [here],
        [(x, None, None) for x in (gq_here, gq_got, go_here, go_got)],
        [((n, cols), bf16, None, None) for n, many in sizes for _ in range(many)],
        [pltpu.VMEM((rows, cols), f32)],
    )
    split = []
    for _, many in sizes:
        split.append(outs[:many])
        outs = outs[many:]
    return split


def sum_of(refs):
    total = refs[0][...].astype(f32)
    for a in refs[1:]:
        total = total + a[...].astype(f32)
    return total


def stage_kernel(jobs, here_ref, *refs):
    n_ins = sum(n for _, n, _ in jobs)
    n_outs = sum(1 << step[1] if kind == "fold" else 1 for kind, _, step in jobs)
    ins, outs, bufs = list(refs[:n_ins]), list(refs[n_ins : n_ins + n_outs]), list(refs[n_ins + n_outs :])
    for kind, n, step in jobs:
        parts, ins = ins[:n], ins[n:]
        if kind == "total":
            outs.pop(0)[...] = sum_of(parts).astype(bf16)
            continue
        bit, many = step[0], 1 << step[1]
        at = (here_ref[0] >> bit) & (many - 1)
        buf = bufs.pop(0)
        if kind == "fold":
            buf[...] = sum_of(parts)
            halves_out(at, buf, outs[:many])
            outs = outs[many:]
        else:
            place(buf, at, parts, 0)
            outs.pop(0)[...] = buf[...].astype(bf16)


def stage(here, *jobs, free=False, after=()):
    outs, scratch, counts = [], [], []
    for kind, parts, step in jobs:
        rows, cols = parts[0].shape
        many = 1 << step[1] if kind == "fold" else 1
        if kind == "fold":
            outs += [((rows // many, cols), bf16, None, None)] * many
            scratch.append(pltpu.VMEM((rows, cols), f32))
        elif kind == "total":
            outs.append(((rows, cols), bf16, None, None))
        else:
            outs.append(((len(parts) * rows, cols), bf16, None, None))
            scratch.append(pltpu.VMEM((len(parts) * rows, cols), f32))
        counts.append(many)
    results = call(
        functools.partial(stage_kernel, [(kind, len(parts), step) for kind, parts, step in jobs]), "stage", (1,),
        [here], [(p, None, None) for _, parts, _ in jobs for p in parts], outs, scratch, free=free, after=after,
    )
    split = []
    for n in counts:
        split.append(results[:n] if n > 1 else results[0])
        results = results[n:]
    return split


class Chain:
    def __init__(self, parts, order, size):
        self.order, self.size, self.step = order, size, 0
        self.last = len(order) - 1
        self.end = 2 * self.last + 1
        self.send(parts)

    def now(self, step):
        return self.order[step if step <= self.last else self.end - step]

    def send(self, parts):
        bit, _ = self.now(self.step)
        self.parts = [parts[0]] + [across(x, m << bit, self.size) for m, x in enumerate(parts[1:], 1)]

    def job(self):
        if self.step < self.last:
            return ("fold", self.parts, self.order[self.step + 1])
        if self.step == self.last:
            return ("total", self.parts, (0, 0))
        return ("join", self.parts, self.now(self.step))

    def take(self, result):
        self.step += 1
        if self.step > self.last:
            result = [result] * (1 << self.now(self.step)[1])
        self.send(result)


def advance(here, *chains, free=False, after=()):
    for chain, result in zip(chains, stage(here, *[c.job() for c in chains], free=free, after=after)):
        chain.take(result)


def plain_sum(at, parts):
    whole = jnp.stack([lax.dynamic_index_in_dim(jnp.stack(parts), at ^ m, 0, False) for m in range(len(parts))])
    whole = lax.psum(whole, "dp")
    return [lax.dynamic_index_in_dim(whole, at ^ m, 0, False) for m in range(len(parts))]


def place(buf, at, parts, low):
    rows = parts[0].shape[0]
    for m, q in enumerate(parts):
        buf[pl.ds(pl.multiple_of(low + (at ^ m) * rows, 8), rows), :] = q[...].astype(buf.dtype)


def end_kernel(at_ref, mine, theirs, out):
    mine_now = pl.program_id(0) // 2 == at_ref[0]
    rows = out.shape[0]
    low = pl.multiple_of(pl.program_id(0) % 2 * rows, 16)

    @pl.when(mine_now)
    def _():
        out[...] = mine[pl.ds(low, rows), :].astype(f32)

    @pl.when(jnp.logical_not(mine_now))
    def _():
        out[...] = theirs[pl.ds(low, rows), :].astype(f32)


def end(at, halves, name):
    rows, cols = halves[0].shape
    return call(
        end_kernel, name, (4,), [at], [(q, None, None) for q in halves],
        [((2 * rows, cols), f32, (rows // 2, cols), lambda i, s: (i, 0))],
        free=True,
    )[0]


def last_end_kernel(steps, here_ref, *refs):
    *parts, qkv_ref, vec_ref, out_ref, buf = refs
    low = 0
    for bit, width in steps:
        many = 1 << width
        place(buf, (here_ref[0] >> bit) & (many - 1), parts[:many], low)
        low += many * parts[0].shape[0]
        parts = parts[many:]
    rows, cols = qkv_ref.shape[1:]
    for c in range(3):
        qkv_ref[c] = buf[c * rows : (c + 1) * rows, :]
    vec_ref[...] = buf[3 * rows : 3 * rows + 16, :]
    half = out_ref.shape[0]
    low = buf.shape[0] - 2 * half
    for side in range(2):
        out_ref[:, side * cols : side * cols + cols] = buf[low + side * half : low + (side + 1) * half, :]


def last_end(here, bands, steps, half):
    rows = sum(len(b) * b[0].shape[0] for b in bands)
    cols = bands[0][0].shape[1]
    return call(
        functools.partial(last_end_kernel, steps), "last_end", (1,), [here], [(q, None, None) for b in bands for q in b],
        [((3, 2 * cols, cols), f32, None, None), ((16, cols), f32, None, None), ((half, 2 * cols), f32, None, None)],
        [pltpu.VMEM((rows, cols), f32)],
        free=True,
    )


def contrast(pooled_all, pool_w, pool_bias, log_temp, pairs_all):
    squash_float = jnp.tanh(dot_nn(pooled_all, pool_w) + pool_bias)
    squash = squash_float.astype(bf16).astype(f32)
    inv_norm = lax.rsqrt(jnp.sum(squash * squash, axis=-1, keepdims=True) + 1e-06)
    unit_all = squash * inv_norm
    temp = jnp.exp(-log_temp[0])
    logits = jnp.dot(unit_all, unit_all.T, precision=highest) * temp
    ids = jnp.arange(pooled_all.shape[0], dtype=jnp.int32)
    masked = jnp.where(ids[None, :] == ids[:, None], -1e30, logits)
    row_top = jnp.max(masked, axis=-1, keepdims=True)
    row_expo = jnp.exp(masked - row_top)
    row_total = jnp.sum(row_expo, axis=-1, keepdims=True)
    chosen = (ids[None, :] == pairs_all[:, None]).astype(f32)
    row_lse = row_top[:, 0] + jnp.log(row_total[:, 0])
    loss_total = jnp.sum(row_lse - jnp.sum(chosen * logits, axis=-1))
    grad_logits = row_expo / row_total - chosen
    grad_temp = -jnp.sum(grad_logits * logits)
    grad_unit = jnp.dot(grad_logits + grad_logits.T, unit_all, precision=highest) * temp
    grad_squash = inv_norm * (
        grad_unit - unit_all * jnp.sum(unit_all * grad_unit, axis=-1, keepdims=True)
    )
    grad_pool_pre = (grad_squash * (1.0 - squash_float * squash_float)).astype(bf16)
    return loss_total, grad_temp, grad_pool_pre


def contrast_kernel(
    count, rank_ref, me_ref, all_here, all_there, w_here, w_there, bias_ref, temp_ref, gw_ref, gb_ref,
    gp_ref, scalars_ref, all_ref, w_ref, pooled_ref, grad_ref,
):
    batch, width = pooled_ref.shape
    half = w_here.shape[0]
    me = me_ref[0]
    w_ref[pl.ds(pl.multiple_of(me * half, 128), half), :] = w_here[...]
    w_ref[pl.ds(pl.multiple_of((1 - me) * half, 128), half), :] = w_there[...]
    block = all_here.shape[0]
    rows_all = all_ref.shape[0]
    place(all_ref, me, (all_here, all_there), 0)
    at = lax.broadcasted_iota(jnp.int32, (batch, rows_all), 1)
    row = lax.broadcasted_iota(jnp.int32, (batch, rows_all), 0)
    base = (row // count % 2) * block + (row // count // 2) * 16
    pooled = dot_nn((at == base + row % count).astype(bf16), all_ref[...]).astype(bf16)
    pooled_ref[...] = pooled
    upper = dot_nn((at == base + count).astype(bf16), all_ref[:, :128])
    lower = dot_nn((at == base + count + 1).astype(bf16), all_ref[:, :128])
    lane = lax.broadcasted_iota(jnp.int32, (batch, 128), 1)
    line = lax.broadcasted_iota(jnp.int32, (batch, 128), 0)
    partner = jnp.sum(jnp.where(lane == line % count, upper * 64.0 + lower, 0.0), axis=1, keepdims=True)
    squash_float = jnp.tanh(dot_nn(pooled, w_ref[...]) + bias_ref[...])
    squash = squash_float.astype(bf16).astype(f32)
    inv_norm = lax.rsqrt(jnp.sum(squash * squash, axis=-1, keepdims=True) + 1e-06)
    unit = squash * inv_norm
    temp = jnp.exp(-temp_ref[0:1, 0:1])
    logits = dot_nt(unit, unit, precision=highest) * temp
    ids = lax.broadcasted_iota(jnp.int32, (batch, batch), 1)
    masked = jnp.where(ids == lax.broadcasted_iota(jnp.int32, (batch, batch), 0), -1e30, logits)
    row_top = jnp.max(masked, axis=-1, keepdims=True)
    row_expo = jnp.exp(masked - row_top)
    row_total = jnp.sum(row_expo, axis=-1, keepdims=True)
    chosen = (ids.astype(f32) == partner).astype(f32)
    row_loss = row_top + jnp.log(row_total) - jnp.sum(chosen * logits, axis=-1, keepdims=True)
    loss = jnp.sum(row_loss, axis=0, keepdims=True) / batch
    grad_logits = row_expo / row_total - chosen
    grad_temp = -jnp.sum(jnp.sum(grad_logits * logits, axis=-1, keepdims=True), axis=0, keepdims=True)
    grad_unit = jnp.dot(
        grad_logits + grad_logits.T, unit, precision=highest, preferred_element_type=f32
    ) * temp
    grad_squash = inv_norm * (grad_unit - unit * jnp.sum(unit * grad_unit, axis=-1, keepdims=True))
    grad_pre = (grad_squash * (1.0 - squash_float * squash_float)).astype(bf16)
    gw_ref[...] = dot_tn(pooled_ref[:, lanes_of(me, half)], grad_pre)
    gb_ref[...] = jnp.sum(grad_pre.astype(f32), axis=0, keepdims=True)
    grad_ref[...] = grad_pre.astype(f32)
    own = grad_ref[pl.ds(pl.multiple_of(rank_ref[0] * count, 8), count), :].astype(bf16)
    gp_ref[...] = dot_nt(own, w_ref[...])
    spot = lax.broadcasted_iota(jnp.int32, (8, 128), 1)
    scalars_ref[...] = jnp.where(spot == 0, loss, grad_temp)


def contrast_call(rank, me, gathered, w_here, w_there, bias, log_temp, count):
    width = w_here.shape[1]
    rows_all = 2 * gathered[0].shape[0]
    batch = rows_all // 16 * count
    half = w_here.shape[0]
    temp = jnp.broadcast_to(log_temp.reshape(1, 1), (8, 128))
    return call(
        functools.partial(contrast_kernel, count), "contrast", (1,), [rank, me],
        [(a, None, None) for a in (*gathered, w_here, w_there, bias.reshape(1, width), temp)],
        [
            ((half, width), f32, None, None),
            ((1, width), f32, None, None),
            ((count, width), f32, None, None),
            ((8, 128), f32, None, None),
        ],
        [
            pltpu.VMEM((rows_all, width), bf16),
            pltpu.VMEM((width, width), bf16),
            pltpu.VMEM((batch, width), bf16),
            pltpu.VMEM((batch, width), f32),
        ],
    )


def per_device(
    dp_size,
    tokens,
    qkv_weight,
    qv_bias,
    out_weight,
    out_bias,
    first_gain,
    first_shift,
    up_weight,
    up_bias,
    down_weight,
    down_bias,
    second_gain,
    second_shift,
    pool_weight,
    pool_bias,
    log_temp,
    segments,
    cls_pos,
    pair_index,
    attn_keep,
    ffn_keep,
    grad_out,
):
    me = lax.axis_index("tensor")
    here = lax.axis_index("dp")
    length = segments.shape[1]
    half = tokens.shape[1]
    units = up_bias.shape[0]
    me_one = me.reshape(1).astype(jnp.int32)
    ORDER.clear()
    here_one = here.reshape(1).astype(jnp.int32)
    spot = here_one & 3

    def ordered(mine, theirs, axis):
        return jnp.where(
            me == 0,
            jnp.concatenate([mine, theirs], axis),
            jnp.concatenate([theirs, mine], axis),
        )

    x_there = other(their_rows(me_one, [tokens], length)[0])
    qkv_there = other(qkv_weight)
    vec = jnp.concatenate(
        [qv_bias.reshape(-1), up_bias, out_bias, first_gain, first_shift, down_bias, second_gain, second_shift]
    ).reshape(1, -1)
    out_there = other(out_weight)
    up_there = other(up_weight)
    down_there = other(down_weight)
    pool_there = other(pool_weight)

    seg = lax.dynamic_slice_in_dim(segments, me, 1, 0)
    col = jnp.broadcast_to(seg.reshape(length, 1), (length, 128))
    cls = lax.dynamic_slice_in_dim(cls_pos, me, 1, 0).reshape(-1)
    qv_full, up_b, feats = vectors(me_one, vec, other(vec), units, half)

    x, q, k, v = project(me_one, tokens, x_there, qkv_weight, qkv_there, qv_full, length)
    sends = their_rows(me_one, [attn_keep, ffn_keep], length)
    keep1 = (attn_keep, other(sends[0]))
    keep2 = (ffn_keep, other(sends[1]))
    ctx, lse = attend(seg, col, q, k, v, [])
    res, low, act, slope, mixed, lay_mine, lay_theirs, pooled = feed_forward(
        me_one, cls, pair_index, ctx, x, out_weight, out_there, keep1, up_weight, up_there, down_weight, down_there,
        up_b, feats, keep2,
    )
    quick = dp_size == 16
    if quick:
        near = [pooled] + [across(pooled, m, dp_size) for m in (1, 2, 3)]
    go_there = other(their_rows(me_one, [grad_out], length)[0])
    if quick:
        (near,) = stage(here_one, ("join", near, (0, 2)))
        (all_here,) = stage(here_one, ("join", [near] + [across(near, m, dp_size) for m in (4, 8, 12)], (2, 2)))
        all_there = other(all_here)
    pool_rows = cls.shape[0]
    rank = here * 2 + me
    batch = dp_size * 2 * pool_rows
    if quick:
        grad_pool_w, grad_pool_b, grad_pooled, scalars = contrast_call(
            rank.reshape(1), me_one, [all_here, all_there], pool_weight, pool_there,
            pool_bias, log_temp, pool_rows,
        )
        grad_pool_b = grad_pool_b.reshape(-1)
        loss, grad_temp = scalars[0, 0], scalars[0, 1]
    else:
        gathered = lax.all_gather(pooled, ("dp", "tensor"), axis=0, tiled=True)
        pool_w = ordered(pool_weight, pool_there, 0)
        gathered = gathered.reshape(-1, pooled.shape[0], D)
        pooled_all = gathered[:, :pool_rows].reshape(-1, D)
        numbers = gathered[:, pool_rows : pool_rows + 2, :pool_rows].astype(jnp.int32)
        pairs_all = (numbers[:, 0] * 64 + numbers[:, 1]).reshape(-1)
        loss_total, grad_temp, grad_pool_pre = contrast(pooled_all, pool_w, pool_bias, log_temp, pairs_all)
        loss = loss_total / batch
        pooled_half = lax.dynamic_slice_in_dim(pooled_all, me * half, half, 1)
        grad_pool_w = dot_tn(pooled_half, grad_pool_pre)
        grad_pool_b = jnp.sum(grad_pool_pre, axis=0, dtype=f32)
        grad_pooled = dot_nt(lax.dynamic_slice_in_dim(grad_pool_pre, rank * pool_rows, pool_rows, 0), pool_w)

    layer_out = both_rows(me_one, lay_mine, other(lay_theirs))
    g, gm, sums2, gd_there = down_back(
        me_one, cls, mixed, grad_out, go_there, grad_pooled, feats, keep2, act
    )
    bit0, bit1 = here_one & 1, (here_one >> 1) & 1
    part, bias_there, gu_there = up_back(bit1, low, g, slope, up_there, down_there, False)
    down = down_own(bit0, act, g, other(gd_there))
    if quick:
        down = Chain(down, ((0, 1), (1, 1), (2, 1), (3, 1)), dp_size)
    part, bias_here, *up = up_back(bit1, low, g, slope, up_weight, down_weight, True, part, other(gu_there))
    if quick:
        up = Chain(up, ((1, 1), (0, 1), (2, 1), (3, 1)), dp_size)
    gr, grad_ctx, delta, sums1, go_there, go_here = out_back(
        me_one, gm, part, res, ctx, keep1, out_weight, out_there, feats, []
    )
    go_got = other(go_there)
    if quick:
        advance(here_one, down)
    grads = attend_back(seg, col, q, k, v, grad_ctx, lse, delta, tuple(range(D // PAIR)), [])
    if quick:
        advance(here_one, down, up)
    gq_there, gq_here = qkv_last(me_one, x, grads, bias_here, bias_there, sums1, sums2)
    rows = gq_here.shape[0] + D
    orders = [((0, 1), (1, 1), (2, 1), (3, 1)), ((1, 1), (0, 1), (2, 1), (3, 1))]
    firsts = [order[0] for order in orders]
    last = last_parts(
        here_one, gq_here, other(gq_there), go_here, go_got, list(zip([rows // 256 * 128, rows], firsts))
    )
    if quick:
        last = [Chain(parts, order, dp_size) for parts, order in zip(last, orders)]
    gt_mine, gt_theirs = tokens_back(me_one, gr, grads, qkv_weight, qkv_there)
    if quick:
        marks = [last[0].parts[0]]
        for c in last:
            advance(here_one, c, free=True, after=[gt_mine])
        marks.append(last[0].parts[0])
        while any(c.step < c.end for c in last):
            for c in last:
                advance(here_one, c, free=True)
            marks.append(last[0].parts[0])
        for chain, waits in ((down, [1]), (up, [1])):
            for wait in waits:
                if chain.step < chain.end:
                    after = [marks[min(wait, len(marks) - 1)]] if wait >= 0 else []
                    advance(here_one, chain, free=True, after=after)
            while chain.step < chain.end:
                advance(here_one, chain, free=True)
        down, up = down.parts, up.parts
        last = [chain.parts for chain in last]
    else:
        down, up = plain_sum(bit0[0], down), plain_sum(bit1[0], up)
        last = [plain_sum((here >> bit) & ((1 << width) - 1), parts) for parts, (bit, width) in zip(last, firsts)]
    grad_tokens = both_rows(me_one, gt_mine, other(gt_theirs))
    g_down_w = end(bit0, down, "down_end")
    g_up_w = end(bit1, up, "up_end")
    g_qkv_w, vec_sum, g_out_w = last_end(here_one, last, firsts, half)
    n_up = units // half
    return (
        layer_out,
        loss.reshape(1),
        grad_tokens,
        g_qkv_w,
        vec_sum[:2],
        g_out_w,
        vec_sum[2 + n_up],
        vec_sum[3 + n_up],
        vec_sum[4 + n_up],
        g_up_w,
        vec_sum[2 : 2 + n_up].reshape(-1),
        g_down_w,
        vec_sum[5 + n_up],
        vec_sum[6 + n_up],
        vec_sum[7 + n_up],
        grad_pool_w,
        grad_pool_b,
        grad_temp.reshape(1),
    )


def solution(mesh):
    return jax.shard_map(
        functools.partial(per_device, mesh.shape["dp"]),
        mesh=mesh,
        in_specs=(
            P("dp", "tensor"),
            P(None, None, "tensor"),
            P(None, "tensor"),
            P("tensor", None),
            P("tensor"),
            P("tensor"),
            P("tensor"),
            P(None, "tensor"),
            P("tensor"),
            P("tensor", None),
            P("tensor"),
            P("tensor"),
            P("tensor"),
            P("tensor", None),
            P(),
            P(),
            P("dp", None),
            P("dp", None),
            P("dp"),
            P("dp", "tensor"),
            P("dp", "tensor"),
            P("dp", "tensor"),
        ),
        out_specs=(
            P("dp", "tensor"),
            P(),
            P("dp", "tensor"),
            P(None, None, "tensor"),
            P(None, "tensor"),
            P("tensor", None),
            P("tensor"),
            P("tensor"),
            P("tensor"),
            P(None, "tensor"),
            P("tensor"),
            P("tensor", None),
            P("tensor"),
            P("tensor"),
            P("tensor"),
            P("tensor", None),
            P(),
            P(),
        ),
        check_vma=False,
    )
```
